128 devices in a mesh: fsdp: 32 (over y_lo, x, z), replica: 4 (over y_hi, core).
Axes of the slice: x: 4, y: 4 (y_hi: 2, y_lo: 2; y = y_hi * 2 + y_lo), z: 4, core: 2. Of those that a mesh axis runs over, the one named last changes fastest.
Arguments:
- tokens: bfloat16 [4, 16384, 2304], P('replica', 'fsdp'), may hold values from -6 to 6
- token_ids: int32 [4, 16384], P('replica', 'fsdp'), may hold values from 2 to 255999, as said below
- cotangent: bfloat16 [4, 16384, 2304], P('replica', 'fsdp'), may hold values from -6 to 6
- norm_gain: float32 [2304], replicated, may hold values from 0.1 to 1.9
- post_gain: float32 [2304], replicated, may hold values from 0.1 to 1.9
- local_qkv: bfloat16 [4, 2304, 2048], P('replica', 'fsdp'), may hold values from -2 to 2
- local_out: bfloat16 [4, 1024, 2304], P('replica', 'fsdp'), may hold values from -1 to 1
- anchor_qkv: float32 [2304, 2048], P('fsdp'), may hold values from -2 to 2
- anchor_out: float32 [1024, 2304], P('fsdp'), may hold values from -1 to 1
- first_qkv: float32 [4, 2304, 2048], P('replica', 'fsdp'), may hold values from -0.078125 to 0.078125
- first_out: float32 [4, 1024, 2304], P('replica', 'fsdp'), may hold values from -0.078125 to 0.078125
- second_qkv: float32 [4, 2304, 2048], P('replica', 'fsdp'), may hold values from 1e-05 to 0.0001
- second_out: float32 [4, 1024, 2304], P('replica', 'fsdp'), may hold values from 1e-05 to 0.0001
- outer_qkv: float32 [2304, 2048], P('fsdp'), may hold values from -0.078125 to 0.078125
- outer_out: float32 [1024, 2304], P('fsdp'), may hold values from -0.078125 to 0.078125
Outputs:
- grad_tokens: bfloat16 [4, 16384, 2304], P('replica', 'fsdp')
- next_first_qkv: float32 [4, 2304, 2048], P('replica', 'fsdp')
- next_first_out: float32 [4, 1024, 2304], P('replica', 'fsdp')
- next_second_qkv: float32 [4, 2304, 2048], P('replica', 'fsdp')
- next_second_out: float32 [4, 1024, 2304], P('replica', 'fsdp')
- next_anchor_qkv: float32 [2304, 2048], P('fsdp')
- next_anchor_out: float32 [1024, 2304], P('fsdp')
- next_outer_qkv: float32 [2304, 2048], P('fsdp')
- next_outer_out: float32 [1024, 2304], P('fsdp')
The draws below stay inside these ranges and needn't reach their ends.
Inputs may be any that keep to these rules, and one draw needn't show every extreme that they name: `token_ids`: A position holding 2 begins a document; the first position of every sequence of 256 tokens holds 2; every other id is 3 or more.
All inputs are finite; a program needn't handle non-finite values.
Results may differ from the reference program's by a relative error of at most 0.03.
The reference program's roundings to bfloat16 on the way (of `hidden`, `heads`, `chances`, `mixture`, `grad_proj`, `grad_mix` and `grad_heads`) count: a program that leaves them out, or rounds other values in their place, can miss the bound.
Values may be sent and summed in bfloat16 or wider, within the bound.
No kernel may reach another device: no remote copies, remote signals or barrier semaphores. Data moves between devices by JAX's collectives and lax.ppermute only.
A program may use at most 128 MiB of HBM per device.

```python
import math
import jax
import jax.numpy as jnp
from jax import lax

D = 2304
HD = 256
QH = 4
KH = 2
SEQ = 256
SYNC_EVERY = 16
TOK_DEV = 512
TOKENS = 16384
REPLICAS = 4
QW = 1024
KW = 512
QKV = 2048
N_FSDP = 32
N_REPLICA = 4


vocab_limit = 256000


score_gain = 3.0


def column_scale():
    columns = jnp.arange(QKV)
    return jnp.where(columns < QW + KW, score_gain, 1.0).astype(jnp.float32)[None, :]


def shared_qkv(key):
    inner_key = jax.random.fold_in(key, 21)
    return jax.random.truncated_normal(inner_key, -4.0, 4.0, (D, QKV), jnp.float32) * D ** (-0.5) * column_scale()


def shared_out(key):
    inner_key = jax.random.fold_in(key, 22)
    return jax.random.truncated_normal(inner_key, -4.0, 4.0, (QW, D), jnp.float32) * QW ** (-0.5)


def draw_anchor_qkv(key, part):
    return shared_qkv(key)


def draw_anchor_out(key, part):
    return shared_out(key)


def draw_local_qkv(key, part):
    base = shared_qkv(key)
    key = jax.random.fold_in(key, 4)
    drift = jax.random.truncated_normal(key, -4.0, 4.0, (REPLICAS, D, QKV), jnp.float32) * (0.25 * D ** (-0.5)) * column_scale()[None]
    return (base[None] + drift).astype(jnp.bfloat16)


def draw_local_out(key, part):
    base = shared_out(key)
    key = jax.random.fold_in(key, 5)
    drift = jax.random.truncated_normal(key, -4.0, 4.0, (REPLICAS, QW, D), jnp.float32) * (0.25 * QW ** (-0.5))
    return (base[None] + drift).astype(jnp.bfloat16)


def draw_token_ids(key, part):
    key = jax.random.fold_in(key, 7)
    id_key, start_key = jax.random.split(key)
    drawn_ids = jax.random.randint(id_key, (REPLICAS, TOKENS), 3, vocab_limit)
    starts = jax.random.randint(start_key, (REPLICAS, TOKENS), 0, 64) == 0
    places = jnp.arange(TOKENS)
    leading = (places % SEQ == 0)[None, :]
    topmost = (places == 1)[None, :]
    ids = jnp.where(starts | leading, 2, drawn_ids)
    ids = jnp.where(topmost, vocab_limit - 1, ids)
    return ids.astype(jnp.int32)


def block_levels(rng, shape, cuts, low, high):
    factor_of = 1.0
    for position, shards_of in cuts:
        heights = jax.random.uniform(jax.random.fold_in(jax.random.fold_in(rng, 6), position), (shards_of,), jnp.float32, low / len(cuts), high / len(cuts))
        factor_of = factor_of * jnp.repeat(jnp.exp(heights), shape[position] // shards_of).reshape((-1,) + (1,) * (len(shape) - 1 - position))
    return factor_of


def bell_draw(key, extent, width, most, cuts=(), kind=jnp.bfloat16):
    loudness = block_levels(key, extent, cuts, -0.22, 0.18) if cuts else 1.0
    drawn = jax.random.normal(key, extent, jnp.float32) * width * loudness
    return jnp.minimum(jnp.maximum(drawn, -most), most).astype(kind)


def setup_inputs(seed: int = 0) -> dict:
    key_of = jax.random.split(jax.random.key(seed), 16)
    tokens = bell_draw(key_of[0], (REPLICAS, TOKENS, D), 1.0, 6.0, ((0, 4), (1, 32)))
    token_ids = draw_token_ids(jax.random.fold_in(key_of[15], 71), 0)
    cotangent = bell_draw(key_of[2], (REPLICAS, TOKENS, D), 1.0, 6.0, ((0, 4), (1, 32)))
    norm_gain = jnp.clip(1.0 + 0.18 * jax.random.normal(key_of[3], (D,), jnp.float32), 0.1, 1.9)
    post_gain = jnp.clip(1.0 + 0.18 * jax.random.normal(key_of[4], (D,), jnp.float32), 0.1, 1.9)
    local_qkv = draw_local_qkv(jax.random.fold_in(key_of[15], 71), 0)
    local_out = draw_local_out(jax.random.fold_in(key_of[15], 71), 0)
    anchor_qkv = draw_anchor_qkv(jax.random.fold_in(key_of[15], 71), 0)
    anchor_out = draw_anchor_out(jax.random.fold_in(key_of[15], 71), 0)
    first_qkv = bell_draw(key_of[9], (REPLICAS, D, QKV), 0.005, 0.078125, ((0, 4), (1, 32)), jnp.float32)
    first_out = bell_draw(key_of[10], (REPLICAS, QW, D), 0.005, 0.078125, ((0, 4), (1, 32)), jnp.float32)
    second_qkv = jnp.clip(jnp.exp(math.log(0.0001) - 2.3025851 * jax.random.uniform(key_of[11], (REPLICAS, D, QKV), jnp.float32) ** block_levels(key_of[11], (REPLICAS, D, QKV), ((0, 4), (1, 32)), -0.2, 0.2)), 9.999999747378752e-06, 0.0001)
    second_out = jnp.clip(jnp.exp(math.log(0.0001) - 2.3025851 * jax.random.uniform(key_of[12], (REPLICAS, QW, D), jnp.float32) ** block_levels(key_of[12], (REPLICAS, QW, D), ((0, 4), (1, 32)), -0.2, 0.2)), 9.999999747378752e-06, 0.0001)
    outer_qkv = bell_draw(key_of[13], (D, QKV), 0.005, 0.078125, ((0, 32),), jnp.float32)
    outer_out = bell_draw(key_of[14], (QW, D), 0.005, 0.078125, ((0, 32),), jnp.float32)
    return dict(tokens=tokens, token_ids=token_ids, cotangent=cotangent, norm_gain=norm_gain, post_gain=post_gain, local_qkv=local_qkv, local_out=local_out, anchor_qkv=anchor_qkv, anchor_out=anchor_out, first_qkv=first_qkv, first_out=first_out, second_qkv=second_qkv, second_out=second_out, outer_qkv=outer_qkv, outer_out=outer_out)


EPS_NORM = 1e-06
SOFTCAP = 50.0
ROPE_BASE = 10000.0
BETA_ONE = 0.9
BETA_TWO = 0.95
EPS_ADAM = 1e-08
INNER_LR = 0.001
DECAY = 0.1
OUTER_LR = 0.7
MOMENTUM = 0.9
START_ID = 2

def narrow(values):
    return lax.optimization_barrier(values.astype(jnp.bfloat16)).astype(jnp.float32)

def normalize(values, gain):
    return values * lax.rsqrt(lax.optimization_barrier(jnp.mean(values * values, axis=-1, keepdims=True)) + EPS_NORM) * gain

def rotate(heads, positions):
    half = heads.shape[-1] // 2
    freqs = ROPE_BASE ** (-2.0 * jnp.arange(half, dtype=jnp.float32) / heads.shape[-1])
    angles = positions[:, None] * freqs[None, :]
    cosine = jnp.cos(angles)[:, None, :]
    sine = jnp.sin(angles)[:, None, :]
    first_half = heads[..., :half]
    second_half = heads[..., half:]
    return jnp.concatenate([first_half * cosine - second_half * sine, second_half * cosine + first_half * sine], axis=-1)

def document_mask(token_rows):
    starts = (token_rows == START_ID).astype(jnp.int32).reshape(-1, SEQ)
    number = jnp.cumsum(starts, axis=1)
    same_doc = number[:, :, None] == number[:, None, :]
    causal = jnp.arange(SEQ)[None, :] <= jnp.arange(SEQ)[:, None]
    return (same_doc & causal[None]).astype(jnp.float32)[:, None, None]

def attend(packed, doc_mask):
    count = packed.shape[0]
    seqs_here = count // SEQ
    group = QH // KH
    width_q = QH * HD
    width_k = KH * HD
    positions = (jnp.arange(count) % SEQ).astype(jnp.float32)
    queries = narrow(rotate(packed[:, :width_q].reshape(count, QH, HD), positions))
    keys_rot = narrow(rotate(packed[:, width_q:width_q + width_k].reshape(count, KH, HD), positions))
    value_rows = narrow(packed[:, width_q + width_k:])
    queries = queries.reshape(seqs_here, SEQ, KH, group, HD)
    keys_rot = keys_rot.reshape(seqs_here, SEQ, KH, HD)
    value_rows = value_rows.reshape(seqs_here, SEQ, KH, HD)
    scores = jnp.einsum('sigrd,sjgd->sgrij', queries, keys_rot) * HD ** (-0.5)
    scores = SOFTCAP * jnp.tanh(scores / SOFTCAP)
    weights = jnp.exp(scores) * doc_mask
    chances = narrow(weights / lax.optimization_barrier(jnp.sum(weights, axis=-1, keepdims=True)))
    mixture = jnp.einsum('sgrij,sjgd->sigrd', chances, value_rows)
    return mixture.reshape(count, width_q).astype(jnp.bfloat16)

def layer_block(inputs, token_rows, upstream_rows, weights_qkv, weights_out, norm_gain, post_gain):
    upstream = upstream_rows.astype(jnp.float32)
    doc_mask = document_mask(token_rows)
    normed, pre_back = jax.vjp(lambda values: normalize(values, norm_gain), inputs.astype(jnp.float32))
    hidden = normed.astype(jnp.bfloat16)
    packed = jnp.dot(hidden, weights_qkv, preferred_element_type=jnp.float32)
    mixture, core_back = jax.vjp(lambda values: attend(values, doc_mask), packed)
    projected = jnp.dot(mixture, weights_out, preferred_element_type=jnp.float32)
    post_back = jax.vjp(lambda values: normalize(values, post_gain), projected)[1]
    grad_proj = post_back(upstream)[0].astype(jnp.bfloat16)
    part_out = lax.dot_general(mixture, grad_proj, (((0,), (0,)), ((), ())), preferred_element_type=jnp.float32)
    grad_mix = lax.dot_general(grad_proj, weights_out, (((1,), (1,)), ((), ())), preferred_element_type=jnp.float32).astype(jnp.bfloat16)
    grad_heads = core_back(grad_mix)[0].astype(jnp.bfloat16)
    part_qkv = lax.dot_general(hidden, grad_heads, (((0,), (0,)), ((), ())), preferred_element_type=jnp.float32)
    grad_hidden = lax.dot_general(grad_heads, weights_qkv, (((1,), (1,)), ((), ())), preferred_element_type=jnp.float32)
    grad_rows = (upstream + pre_back(grad_hidden)[0]).astype(jnp.bfloat16)
    return (grad_rows, part_qkv, part_out)

def adam_step(weights, grads, first, second, steps_done):
    first_next = BETA_ONE * first + (1.0 - BETA_ONE) * grads
    second_next = BETA_TWO * second + (1.0 - BETA_TWO) * grads * grads
    first_hat = first_next / (1.0 - BETA_ONE ** steps_done)
    second_hat = second_next / (1.0 - BETA_TWO ** steps_done)
    master = weights.astype(jnp.float32)
    inner = master - INNER_LR * (first_hat / (jnp.sqrt(second_hat) + EPS_ADAM) + DECAY * master)
    return (inner, first_next, second_next)

def reference(tokens, token_ids, cotangent, norm_gain, post_gain, local_qkv, local_out, anchor_qkv, anchor_out, first_qkv, first_out, second_qkv, second_out, outer_qkv, outer_out):
    steps_done = float(SYNC_EVERY)
    grad_list, firsts_qkv, firsts_out, seconds_qkv, seconds_out = ([], [], [], [], [])
    pseudo_qkv = jnp.zeros((D, QKV), jnp.float32)
    pseudo_out = jnp.zeros((QW, D), jnp.float32)
    for replica in range(N_REPLICA):
        blocks = (tokens[replica].reshape(N_FSDP, TOK_DEV, D), token_ids[replica].reshape(N_FSDP, TOK_DEV), cotangent[replica].reshape(N_FSDP, TOK_DEV, D))

        def visit(carry, block, replica=replica):
            grad_rows, part_qkv, part_out = layer_block(block[0], block[1], block[2], local_qkv[replica], local_out[replica], norm_gain, post_gain)
            return ((carry[0] + narrow(part_qkv), carry[1] + narrow(part_out)), grad_rows)
        start_sums = (jnp.zeros((D, QKV), jnp.float32), jnp.zeros((QW, D), jnp.float32))
        (sum_qkv, sum_out), grad_rows = lax.scan(visit, start_sums, blocks)
        grad_list.append(grad_rows.reshape(TOKENS, D))
        inner_qkv, first_q, second_q = adam_step(local_qkv[replica], sum_qkv / TOKENS, first_qkv[replica], second_qkv[replica], steps_done)
        inner_out, first_o, second_o = adam_step(local_out[replica], sum_out / TOKENS, first_out[replica], second_out[replica], steps_done)
        firsts_qkv.append(first_q)
        firsts_out.append(first_o)
        seconds_qkv.append(second_q)
        seconds_out.append(second_o)
        pseudo_qkv = pseudo_qkv + (anchor_qkv - inner_qkv)
        pseudo_out = pseudo_out + (anchor_out - inner_out)
    pseudo_qkv = pseudo_qkv / N_REPLICA
    pseudo_out = pseudo_out / N_REPLICA
    outer_next_qkv = MOMENTUM * outer_qkv + pseudo_qkv
    outer_next_out = MOMENTUM * outer_out + pseudo_out
    anchor_next_qkv = anchor_qkv - OUTER_LR * (pseudo_qkv + MOMENTUM * outer_next_qkv)
    anchor_next_out = anchor_out - OUTER_LR * (pseudo_out + MOMENTUM * outer_next_out)
    return (jnp.stack(grad_list), jnp.stack(firsts_qkv), jnp.stack(firsts_out), jnp.stack(seconds_qkv), jnp.stack(seconds_out), anchor_next_qkv, anchor_next_out, outer_next_qkv, outer_next_out)
```

```python
import functools

import jax
import jax.numpy as jnp
from jax import lax
from jax.experimental import pallas as pl
from jax.experimental.pallas import tpu as pltpu
from jax.sharding import PartitionSpec as P

HD = 256
SEQ = 256
SYNC_EVERY = 16
TOKENS = 16384

EPS_NORM = 1e-06
SOFTCAP = 50.0
ROPE_BASE = 10000.0
BETA_ONE = 0.9
BETA_TWO = 0.95
EPS_ADAM = 1e-08
INNER_LR = 0.001
DECAY = 0.1
OUTER_LR = 0.7
MOMENTUM = 0.9
START_ID = 2

BF16 = jnp.bfloat16
F32 = jnp.float32


def place(step):
    pairs = []
    for source in range(128):
        y_lo, x, z, y_hi, core = source // 64, source // 16 % 4, source // 4 % 4, source // 2 % 2, source % 2
        y_lo, x, z, y_hi, core = step(y_lo, x, z, y_hi, core)
        pairs.append((source, (((y_lo * 4 + x) * 4 + z) * 2 + y_hi) * 2 + core))
    return pairs


TRADE = place(lambda y, x, z, h, c: (c, x, z, h, y))
TRADE_CROSS = place(lambda y, x, z, h, c: (c, x, z, h, 1 - y))
TRADE_CROSS_BACK = place(lambda y, x, z, h, c: (1 - c, x, z, h, y))
CORE = place(lambda y, x, z, h, c: (y, x, z, h, 1 - c))
FAR = place(lambda y, x, z, h, c: (y, x, z, 1 - h, c))
RING = {
    "x": {d: place(lambda y, x, z, h, c, d=d: (y, (x + d) % 4, z, h, c)) for d in (1, 2, 3)},
    "z": {d: place(lambda y, x, z, h, c, d=d: (y, x, (z + d) % 4, h, c)) for d in (1, 2, 3)},
}


def send(values, pairs):
    return lax.ppermute(values, ("fsdp", "replica"), pairs)


def group_columns(values, group):
    return jnp.concatenate(
        [
            values[:, 512 * group : 512 * group + 512],
            values[:, 1024 + 256 * group : 1280 + 256 * group],
            values[:, 1536 + 256 * group : 1792 + 256 * group],
        ],
        axis=1,
    )


def whole_columns(first, second):
    return jnp.concatenate(
        [
            first[:, :512],
            second[:, :512],
            first[:, 512:768],
            second[:, 512:768],
            first[:, 768:],
            second[:, 768:],
        ],
        axis=1,
    )


def normalize(values, gain):
    return values * lax.rsqrt(jnp.mean(values * values, axis=-1, keepdims=True) + EPS_NORM) * gain


def rope_tables():
    freqs = ROPE_BASE ** (-2.0 * jnp.arange(HD // 2, dtype=F32) / HD)
    angles = jnp.arange(SEQ, dtype=F32)[:, None] * freqs[None, :]
    return jnp.cos(angles), jnp.sin(angles)


def doc_numbers(flags):
    ordered = (jnp.arange(SEQ)[:, None] <= jnp.arange(SEQ)[None, :]).astype(BF16)
    numbers = jnp.dot(flags, ordered, preferred_element_type=F32)
    return numbers[:, None, :], numbers[:, :, None]


def doc_mask(row_ref, col_ref):
    same_doc = col_ref[0] == row_ref[0]
    places = (SEQ, SEQ)
    causal = lax.broadcasted_iota(jnp.int32, places, 1) <= lax.broadcasted_iota(jnp.int32, places, 0)
    return same_doc & causal


def rotated(values, cosine, sine):
    first, second = values[:, : HD // 2], values[:, HD // 2 :]
    return jnp.concatenate(
        [first * cosine - second * sine, second * cosine + first * sine], axis=1
    ).astype(BF16)


def rotated_back(grads, cosine, sine):
    grads = grads.astype(BF16).astype(F32)
    first, second = grads[:, : HD // 2], grads[:, HD // 2 :]
    return jnp.concatenate(
        [first * cosine + second * sine, second * cosine - first * sine], axis=1
    ).astype(BF16)


def dot_nt(left, right):
    return lax.dot_general(left, right, (((1,), (1,)), ((), ())), preferred_element_type=F32)


def dot_tn(left, right):
    return lax.dot_general(left, right, (((0,), (0,)), ((), ())), preferred_element_type=F32)


def chance(query, key, mask):
    capped = jnp.tanh(dot_nt(query, key) * (HD**-0.5 / SOFTCAP))
    weights = jnp.where(mask, jnp.exp(SOFTCAP * capped), 0.0)
    return capped, weights / jnp.sum(weights, axis=1, keepdims=True)


def attention_kernel(packed_ref, row_ref, col_ref, cos_ref, sin_ref, heads_ref, mixture_ref):
    mask = doc_mask(row_ref, col_ref)
    cosine, sine = cos_ref[...], sin_ref[...]
    key = rotated(packed_ref[:, 512:768], cosine, sine)
    value = packed_ref[:, 768:].astype(BF16)
    heads_ref[:, 512:768] = key
    heads_ref[:, 768:] = value
    for head in range(2):
        columns = slice(head * HD, head * HD + HD)
        query = rotated(packed_ref[:, columns], cosine, sine)
        heads_ref[:, columns] = query
        chances = chance(query, key, mask)[1].astype(BF16)
        mixture_ref[:, columns] = jnp.dot(chances, value, preferred_element_type=F32).astype(BF16)


def attention_back_kernel(heads_ref, grad_ref, row_ref, col_ref, cos_ref, sin_ref, out_ref):
    mask = doc_mask(row_ref, col_ref)
    cosine, sine = cos_ref[...], sin_ref[...]
    key, value = heads_ref[:, 512:768], heads_ref[:, 768:]
    grad_key = jnp.zeros((SEQ, HD), F32)
    grad_value = jnp.zeros((SEQ, HD), F32)
    for head in range(2):
        columns = slice(head * HD, head * HD + HD)
        query, grad = heads_ref[:, columns], grad_ref[:, columns]
        capped, chances = chance(query, key, mask)
        grad_chance = dot_nt(grad, value).astype(BF16).astype(F32)
        inner = jnp.sum(grad_chance * chances, axis=1, keepdims=True)
        grad_score = chances * (grad_chance - inner) * (1.0 - capped * capped) * HD**-0.5
        grad_score = grad_score.astype(BF16)
        grad_query = jnp.dot(grad_score, key, preferred_element_type=F32)
        out_ref[:, columns] = rotated_back(grad_query, cosine, sine)
        grad_key += dot_tn(grad_score, query)
        grad_value += dot_tn(chances.astype(BF16), grad)
    out_ref[:, 512:768] = rotated_back(grad_key, cosine, sine)
    out_ref[:, 768:] = grad_value.astype(BF16)


def per_sequence(width):
    return pl.BlockSpec((SEQ, width), lambda s: (s, 0))


DOC_SPECS = [
    pl.BlockSpec((1, 1, SEQ), lambda s: (s, 0, 0)),
    pl.BlockSpec((1, SEQ, 1), lambda s: (s, 0, 0)),
    pl.BlockSpec((SEQ, HD // 2), lambda s: (0, 0)),
    pl.BlockSpec((SEQ, HD // 2), lambda s: (0, 0)),
]
KERNEL_PARAMS = pltpu.CompilerParams(vmem_limit_bytes=32 * 1024 * 1024)


def attention(packed, rows, cols, cosine, sine):
    count = packed.shape[0]
    return pl.pallas_call(
        attention_kernel,
        grid=(count // SEQ,),
        in_specs=[per_sequence(1024)] + DOC_SPECS,
        out_specs=[per_sequence(1024), per_sequence(512)],
        out_shape=[jax.ShapeDtypeStruct((count, 1024), BF16), jax.ShapeDtypeStruct((count, 512), BF16)],
        compiler_params=KERNEL_PARAMS,
        name="attention",
    )(packed, rows, cols, cosine, sine)


def attention_back(heads, grads, rows, cols, cosine, sine):
    count = heads.shape[0]
    return pl.pallas_call(
        attention_back_kernel,
        grid=(count // SEQ,),
        in_specs=[per_sequence(1024), per_sequence(512)] + DOC_SPECS,
        out_specs=per_sequence(1024),
        out_shape=jax.ShapeDtypeStruct((count, 1024), BF16),
        compiler_params=KERNEL_PARAMS,
        name="attention_back",
    )(heads, grads, rows, cols, cosine, sine)


def spread(block, axis, index):
    return [
        (index, block),
        ((index + 3) % 4, send(block, RING[axis][1])),
        ((index + 1) % 4, send(block, RING[axis][3])),
        ((index + 2) % 4, send(block, RING[axis][2])),
    ]


def collect(pick, axis, index):
    total = pick(index).astype(F32)
    for step in (2, 1, 3):
        total = total + send(pick((index + step) % 4), RING[axis][step]).astype(F32)
    return total


def put(whole, block, start):
    return lax.dynamic_update_slice(whole, block, start)


def take(values, axis, index):
    return lax.dynamic_index_in_dim(values, index, axis, keepdims=False)


def gather_qkv(near, cross, x, z, core):
    near_line = jnp.zeros((4, 72, 1024), BF16)
    for index, block in spread(near, "x", x):
        near_line = put(near_line, block[None], (index, 0, 0))
    cross_line = jnp.zeros((4, 72, 1024), BF16)
    for index, block in spread(cross, "z", z):
        cross_line = put(cross_line, block[None], (index, 0, 0))
    whole = jnp.zeros((2, 4, 4, 72, 1024), BF16)
    for index, block in spread(near_line, "z", z):
        whole = put(whole, block[None, :, None], (core, 0, index, 0, 0))
    for index, block in spread(cross_line, "x", x):
        whole = put(whole, block[None, None], (1 - core, index, 0, 0, 0))
    return whole.reshape(2304, 1024)


def reduce_qkv(partial, x, z, core):
    partial = partial.reshape(2, 4, 4, 72, 1024)
    near, cross = take(partial, 0, core), take(partial, 0, 1 - core)
    near_line = collect(lambda index: take(near, 1, index), "z", z).astype(BF16)
    cross_line = collect(lambda index: take(cross, 0, index), "x", x).astype(BF16)
    return (
        collect(lambda index: take(near_line, 0, index), "x", x).astype(BF16),
        collect(lambda index: take(cross_line, 0, index), "z", z).astype(BF16),
    )


def reduce_out(partial, x, z):
    partial = partial.reshape(4, 4, 32, 2304)
    left, right = partial[..., :1152], partial[..., 1152:]
    left_line = collect(lambda index: take(left, 1, index), "z", z).astype(BF16)
    right_line = collect(lambda index: take(right, 0, index), "x", x).astype(BF16)
    return jnp.concatenate(
        [
            collect(lambda index: take(left_line, 0, index), "x", x).astype(BF16),
            collect(lambda index: take(right_line, 0, index), "z", z).astype(BF16),
        ],
        axis=1,
    )


def adam_step(weights, grads, first, second, steps_done):
    first_next = BETA_ONE * first + (1.0 - BETA_ONE) * grads
    second_next = BETA_TWO * second + (1.0 - BETA_TWO) * grads * grads
    first_hat = first_next / (1.0 - BETA_ONE**steps_done)
    second_hat = second_next / (1.0 - BETA_TWO**steps_done)
    master = weights.astype(F32)
    inner = master - INNER_LR * (first_hat / (jnp.sqrt(second_hat) + EPS_ADAM) + DECAY * master)
    return (inner, first_next, second_next)


def over_replicas(change):
    change = change.astype(BF16)
    pair = (change.astype(F32) + send(change, CORE).astype(F32)).astype(BF16)
    return (pair.astype(F32) + send(pair, FAR).astype(F32)) / 4.0


def per_device(
    tokens,
    token_ids,
    cotangent,
    norm_gain,
    post_gain,
    local_qkv,
    local_out,
    anchor_qkv,
    anchor_out,
    first_qkv,
    first_out,
    second_qkv,
    second_out,
    outer_qkv,
    outer_out,
):
    place_fsdp = lax.axis_index("fsdp")
    y_lo, x, z = place_fsdp // 16, place_fsdp // 4 % 4, place_fsdp % 4
    core = lax.axis_index("replica") % 2
    part_qkv, part_out = local_qkv[0], local_out[0]

    flags = (token_ids[0] == START_ID).astype(BF16).reshape(1, 512)
    flags = jnp.pad(flags, ((0, 7), (0, 512)))
    group_a, group_b = group_columns(part_qkv, 0), group_columns(part_qkv, 1)
    near = send(jnp.concatenate([jnp.where(y_lo == 0, group_a, group_b), flags], axis=0), TRADE)
    cross = send(jnp.concatenate([jnp.where(y_lo == 0, group_b, group_a), flags], axis=0), TRADE_CROSS)
    rows_out = send(part_out, TRADE)
    own_tokens = send(tokens[0], TRADE)
    other_tokens = send(own_tokens, CORE)
    upstream = send(cotangent[0], TRADE).astype(F32)

    full_qkv = gather_qkv(near[:72], cross[:72], x, z, core)
    groups = [[16 * y + i for i in range(16)] for y in range(2)]
    own_out = lax.all_gather(rows_out, "fsdp", axis=0, tiled=True, axis_index_groups=groups)
    other_out = send(own_out, CORE)
    full_out = jnp.concatenate([own_out, other_out], axis=0)

    flags = jnp.concatenate([near[72, :512].reshape(2, SEQ), cross[72, :512].reshape(2, SEQ)], axis=0)
    rows, cols = doc_numbers(flags)
    cosine, sine = rope_tables()

    own_normed, pre_back = jax.vjp(lambda values: normalize(values, norm_gain), own_tokens.astype(F32))
    other_normed = normalize(other_tokens.astype(F32), norm_gain)
    hidden = jnp.concatenate([own_normed.astype(BF16), other_normed.astype(BF16)], axis=0)
    packed = jnp.dot(hidden, full_qkv, preferred_element_type=F32)
    heads, mixture = attention(packed, rows, cols, cosine, sine)
    own_mixture = jnp.concatenate([mixture[:512], send(mixture[512:], CORE)], axis=1)
    projected = jnp.dot(own_mixture, full_out, preferred_element_type=F32)

    post_back = jax.vjp(lambda values: normalize(values, post_gain), projected)[1]
    grad_proj = post_back(upstream)[0].astype(BF16)
    grad_mix = dot_nt(grad_proj, full_out).astype(BF16)
    grad_mix = jnp.concatenate([grad_mix[:, :512], send(grad_mix[:, 512:], CORE)], axis=0)
    both_proj = jnp.concatenate([grad_proj, send(grad_proj, CORE)], axis=0)
    sum_out = reduce_out(dot_tn(mixture, both_proj).astype(BF16), x, z)
    grad_heads = attention_back(heads, grad_mix, rows, cols, cosine, sine)
    sum_near, sum_cross = reduce_qkv(dot_tn(hidden, grad_heads).astype(BF16), x, z, core)
    grad_hidden = dot_nt(grad_heads, full_qkv)
    grad_hidden = grad_hidden[:512] + send(grad_hidden[512:].astype(BF16), CORE).astype(F32)
    grad_rows = (upstream + pre_back(grad_hidden)[0]).astype(BF16)
    grad_rows = send(grad_rows, TRADE)

    sum_out = send(sum_out, TRADE).astype(F32)
    sum_near = send(sum_near, TRADE)
    sum_cross = send(sum_cross, TRADE_CROSS_BACK)
    sum_qkv = whole_columns(
        jnp.where(y_lo == 0, sum_near, sum_cross), jnp.where(y_lo == 0, sum_cross, sum_near)
    ).astype(F32)

    steps_done = float(SYNC_EVERY)
    inner_qkv, next_first_qkv, next_second_qkv = adam_step(
        part_qkv, sum_qkv / TOKENS, first_qkv[0], second_qkv[0], steps_done
    )
    inner_out, next_first_out, next_second_out = adam_step(
        part_out, sum_out / TOKENS, first_out[0], second_out[0], steps_done
    )
    pseudo_qkv = over_replicas(anchor_qkv - inner_qkv)
    pseudo_out = over_replicas(anchor_out - inner_out)
    outer_next_qkv = MOMENTUM * outer_qkv + pseudo_qkv
    outer_next_out = MOMENTUM * outer_out + pseudo_out
    anchor_next_qkv = anchor_qkv - OUTER_LR * (pseudo_qkv + MOMENTUM * outer_next_qkv)
    anchor_next_out = anchor_out - OUTER_LR * (pseudo_out + MOMENTUM * outer_next_out)
    return (
        grad_rows[None],
        next_first_qkv[None],
        next_first_out[None],
        next_second_qkv[None],
        next_second_out[None],
        anchor_next_qkv,
        anchor_next_out,
        outer_next_qkv,
        outer_next_out,
    )


def solution(mesh):
    rows = P("replica", "fsdp", None)
    shared = P("fsdp", None)
    in_specs = (rows, P("replica", "fsdp"), rows, P(), P(), rows, rows, shared, shared, rows, rows, rows, rows, shared, shared)
    out_specs = (rows, rows, rows, rows, rows, shared, shared, shared, shared)
    return jax.shard_map(per_device, mesh=mesh, in_specs=in_specs, out_specs=out_specs, check_vma=False)
```

```python
import functools

import jax
import jax.numpy as jnp
from jax import lax
from jax.experimental import pallas as pl
from jax.experimental.pallas import tpu as pltpu
from jax.sharding import PartitionSpec as P

HD = 256
SEQ = 256
SYNC_EVERY = 16
TOKENS = 16384

EPS_NORM = 1e-06
SOFTCAP = 50.0
ROPE_BASE = 10000.0
BETA_ONE = 0.9
BETA_TWO = 0.95
EPS_ADAM = 1e-08
INNER_LR = 0.001
DECAY = 0.1
OUTER_LR = 0.7
MOMENTUM = 0.9
START_ID = 2

BF16 = jnp.bfloat16
F32 = jnp.float32


def place(step):
    pairs = []
    for source in range(128):
        y_lo, x, z, y_hi, core = source // 64, source // 16 % 4, source // 4 % 4, source // 2 % 2, source % 2
        y_lo, x, z, y_hi, core = step(y_lo, x, z, y_hi, core)
        pairs.append((source, (((y_lo * 4 + x) * 4 + z) * 2 + y_hi) * 2 + core))
    return pairs


TRADE = place(lambda y, x, z, h, c: (1 - c, x, z, h, y))
TRADE_BACK = place(lambda y, x, z, h, c: (c, x, z, h, 1 - y))
TRADE_CROSS = place(lambda y, x, z, h, c: (1 - c, x, z, h, 1 - y))
CORE = place(lambda y, x, z, h, c: (y, x, z, h, 1 - c))
FAR = place(lambda y, x, z, h, c: (y, x, z, 1 - h, c))
RING = {
    "x": {d: place(lambda y, x, z, h, c, d=d: (y, (x + d) % 4, z, h, c)) for d in (1, 2, 3)},
    "z": {d: place(lambda y, x, z, h, c, d=d: (y, x, (z + d) % 4, h, c)) for d in (1, 2, 3)},
}


def send(values, pairs):
    return lax.ppermute(values, ("fsdp", "replica"), pairs)


def group_columns(values, group):
    return jnp.concatenate(
        [
            values[:, 512 * group : 512 * group + 512],
            values[:, 1024 + 256 * group : 1280 + 256 * group],
            values[:, 1536 + 256 * group : 1792 + 256 * group],
        ],
        axis=1,
    )


def whole_columns(first, second):
    return jnp.concatenate(
        [
            first[:, :512],
            second[:, :512],
            first[:, 512:768],
            second[:, 512:768],
            first[:, 768:],
            second[:, 768:],
        ],
        axis=1,
    )


def normalize(values, gain):
    return values * lax.rsqrt(jnp.mean(values * values, axis=-1, keepdims=True) + EPS_NORM) * gain


def rope_tables():
    freqs = ROPE_BASE ** (-2.0 * jnp.arange(HD // 2, dtype=F32) / HD)
    angles = jnp.arange(SEQ, dtype=F32)[:, None] * freqs[None, :]
    return jnp.cos(angles), jnp.sin(angles)


def doc_numbers(flags):
    ordered = (jnp.arange(SEQ)[:, None] <= jnp.arange(SEQ)[None, :]).astype(BF16)
    numbers = jnp.dot(flags, ordered, preferred_element_type=F32)
    return numbers[:, None, :], numbers[:, :, None]


def doc_mask(row_ref, col_ref):
    same_doc = col_ref[0] == row_ref[0]
    places = (SEQ, SEQ)
    causal = lax.broadcasted_iota(jnp.int32, places, 1) <= lax.broadcasted_iota(jnp.int32, places, 0)
    return same_doc & causal


def rotated(values, cosine, sine):
    first, second = values[:, : HD // 2], values[:, HD // 2 :]
    return jnp.concatenate(
        [first * cosine - second * sine, second * cosine + first * sine], axis=1
    ).astype(BF16)


def rotated_back(grads, cosine, sine):
    grads = grads.astype(BF16).astype(F32)
    first, second = grads[:, : HD // 2], grads[:, HD // 2 :]
    return jnp.concatenate(
        [first * cosine + second * sine, second * cosine - first * sine], axis=1
    ).astype(BF16)


def dot_nt(left, right):
    return lax.dot_general(left, right, (((1,), (1,)), ((), ())), preferred_element_type=F32)


def dot_tn(left, right):
    return lax.dot_general(left, right, (((0,), (0,)), ((), ())), preferred_element_type=F32)


def chance(query, key, mask):
    capped = jnp.tanh(dot_nt(query, key) * (HD**-0.5 / SOFTCAP))
    weights = jnp.where(mask, jnp.exp(SOFTCAP * capped), 0.0)
    return capped, weights / jnp.sum(weights, axis=1, keepdims=True)


def attention_kernel(packed_ref, row_ref, col_ref, cos_ref, sin_ref, heads_ref, mixture_ref):
    mask = doc_mask(row_ref, col_ref)
    cosine, sine = cos_ref[...], sin_ref[...]
    key = rotated(packed_ref[:, 512:768], cosine, sine)
    value = packed_ref[:, 768:].astype(BF16)
    heads_ref[:, 512:768] = key
    heads_ref[:, 768:] = value
    for head in range(2):
        columns = slice(head * HD, head * HD + HD)
        query = rotated(packed_ref[:, columns], cosine, sine)
        heads_ref[:, columns] = query
        chances = chance(query, key, mask)[1].astype(BF16)
        mixture_ref[:, columns] = jnp.dot(chances, value, preferred_element_type=F32).astype(BF16)


def attention_back_kernel(heads_ref, grad_ref, row_ref, col_ref, cos_ref, sin_ref, out_ref):
    mask = doc_mask(row_ref, col_ref)
    cosine, sine = cos_ref[...], sin_ref[...]
    key, value = heads_ref[:, 512:768], heads_ref[:, 768:]
    grad_key = jnp.zeros((SEQ, HD), F32)
    grad_value = jnp.zeros((SEQ, HD), F32)
    for head in range(2):
        columns = slice(head * HD, head * HD + HD)
        query, grad = heads_ref[:, columns], grad_ref[:, columns]
        capped, chances = chance(query, key, mask)
        grad_chance = dot_nt(grad, value).astype(BF16).astype(F32)
        inner = jnp.sum(grad_chance * chances, axis=1, keepdims=True)
        grad_score = chances * (grad_chance - inner) * (1.0 - capped * capped) * HD**-0.5
        grad_score = grad_score.astype(BF16)
        grad_query = jnp.dot(grad_score, key, preferred_element_type=F32)
        out_ref[:, columns] = rotated_back(grad_query, cosine, sine)
        grad_key += dot_tn(grad_score, query)
        grad_value += dot_tn(chances.astype(BF16), grad)
    out_ref[:, 512:768] = rotated_back(grad_key, cosine, sine)
    out_ref[:, 768:] = grad_value.astype(BF16)


def per_sequence(width):
    return pl.BlockSpec((SEQ, width), lambda s: (s, 0))


DOC_SPECS = [
    pl.BlockSpec((1, 1, SEQ), lambda s: (s, 0, 0)),
    pl.BlockSpec((1, SEQ, 1), lambda s: (s, 0, 0)),
    pl.BlockSpec((SEQ, HD // 2), lambda s: (0, 0)),
    pl.BlockSpec((SEQ, HD // 2), lambda s: (0, 0)),
]
KERNEL_PARAMS = pltpu.CompilerParams(vmem_limit_bytes=32 * 1024 * 1024)


def attention(packed, rows, cols, cosine, sine):
    count = packed.shape[0]
    return pl.pallas_call(
        attention_kernel,
        grid=(count // SEQ,),
        in_specs=[per_sequence(1024)] + DOC_SPECS,
        out_specs=[per_sequence(1024), per_sequence(512)],
        out_shape=[jax.ShapeDtypeStruct((count, 1024), BF16), jax.ShapeDtypeStruct((count, 512), BF16)],
        compiler_params=KERNEL_PARAMS,
        cost_estimate=pl.CostEstimate(flops=6 * count * 1024 * SEQ, bytes_accessed=8 * count * 1024, transcendentals=4 * count * SEQ),
        name="attention",
    )(packed, rows, cols, cosine, sine)


def attention_back(heads, grads, rows, cols, cosine, sine):
    count = heads.shape[0]
    return pl.pallas_call(
        attention_back_kernel,
        grid=(count // SEQ,),
        in_specs=[per_sequence(1024), per_sequence(512)] + DOC_SPECS,
        out_specs=per_sequence(1024),
        out_shape=jax.ShapeDtypeStruct((count, 1024), BF16),
        compiler_params=KERNEL_PARAMS,
        cost_estimate=pl.CostEstimate(flops=12 * count * 1024 * SEQ, bytes_accessed=8 * count * 1024, transcendentals=4 * count * SEQ),
        name="attention_back",
    )(heads, grads, rows, cols, cosine, sine)


def after(values, *others):
    return lax.optimization_barrier((values, *others))[0]


def parts_of(values, axis, index):
    return [lax.dynamic_index_in_dim(values, (index + d) & 3, axis, keepdims=False) for d in range(4)]


def put(whole, block, start):
    return lax.dynamic_update_slice(whole, block, start)


def line_of(block, axis, index):
    line = jnp.zeros((4,) + block.shape, BF16)
    line = put(line, block[None], (index, 0, 0))
    ahead, behind = both_ways(block, axis)
    across = send(after(block, ahead), RING[axis][2])
    for step, received in ((3, ahead), (1, behind), (2, across)):
        line = put(line, received[None], ((index + step) & 3, 0, 0))
    return line


def both_ways(line, axis):
    return send(line, RING[axis][1]), send(line, RING[axis][3])


def send_near(parts, axis):
    return send(parts[1], RING[axis][1]), send(parts[3], RING[axis][3])


def pack_rest(rest):
    return jnp.concatenate([rest[..., 8 * k : 8 * k + 8, :] for k in range(4)], axis=-1)


def unpack_rest(rest):
    return jnp.concatenate([rest[:, 256 * k : 256 * k + 256] for k in range(4)], axis=0)


def add(left, right):
    return (left.astype(F32) + right.astype(F32)).astype(BF16)


def total(*terms):
    return functools.reduce(lambda left, right: left + right, [term.astype(F32) for term in terms]).astype(BF16)


def collect(parts, axis):
    return total(parts[0], *[send(parts[step], RING[axis][step]) for step in (1, 3, 2)])


def adam_step(weights, grads, first, second, steps_done):
    first_next = BETA_ONE * first + (1.0 - BETA_ONE) * grads
    second_next = BETA_TWO * second + (1.0 - BETA_TWO) * grads * grads
    first_hat = first_next / (1.0 - BETA_ONE**steps_done)
    second_hat = second_next / (1.0 - BETA_TWO**steps_done)
    master = weights.astype(F32)
    inner = master - INNER_LR * (first_hat / (jnp.sqrt(second_hat) + EPS_ADAM) + DECAY * master)
    return (inner, first_next, second_next)


def over_replicas(change):
    pair = add(change, send(change, CORE))
    return (pair.astype(F32) + send(pair, FAR).astype(F32)) / 4.0


def per_device(
    tokens,
    token_ids,
    cotangent,
    norm_gain,
    post_gain,
    local_qkv,
    local_out,
    anchor_qkv,
    anchor_out,
    first_qkv,
    first_out,
    second_qkv,
    second_out,
    outer_qkv,
    outer_out,
):
    place_fsdp = lax.axis_index("fsdp")
    y_lo, x, z = place_fsdp >> 4, (place_fsdp >> 2) & 3, place_fsdp & 3
    core = lax.axis_index("replica") & 1
    part_qkv, part_out = local_qkv[0], local_out[0]

    flags = (token_ids[0] == START_ID).astype(BF16).reshape(1, 512)
    flags = jnp.pad(flags, ((0, 7), (0, 512)))
    group_a, group_b = group_columns(part_qkv, 0), group_columns(part_qkv, 1)
    near = send(jnp.concatenate([jnp.where(y_lo == 0, group_a, group_b), flags], axis=0), TRADE)
    cross = send(jnp.concatenate([jnp.where(y_lo == 0, group_b, group_a), flags], axis=0), TRADE_CROSS)
    rows_out = send(part_out, TRADE)
    near, cross, rows_out = lax.optimization_barrier((near, cross, rows_out))

    tokens_a = send(after(tokens[0, :256], near), TRADE)
    near_line = line_of(near[:72], "x", x)
    cross_line = line_of(cross[:72], "z", z)
    near_line, cross_line, tokens_a = lax.optimization_barrier((near_line, cross_line, tokens_a))

    tokens_b = send(after(tokens[0, 256:], tokens_a), TRADE)
    near_up, near_down = both_ways(near_line, "z")
    cross_up, cross_down = both_ways(cross_line, "x")
    own_tokens = jnp.concatenate([tokens_a, tokens_b], axis=0)
    near_line, cross_line, near_up, near_down, cross_up, cross_down, own_tokens = lax.optimization_barrier(
        (near_line, cross_line, near_up, near_down, cross_up, cross_down, own_tokens)
    )

    near_far = send(near_line, RING["z"][2])
    cross_far = send(cross_line, RING["x"][2])
    other_tokens = send(own_tokens, CORE)
    upstream = send(after(cotangent[0], own_tokens), TRADE)
    own_normed, pre_back = jax.vjp(lambda values: normalize(values, norm_gain), own_tokens.astype(F32))
    other_normed = normalize(other_tokens.astype(F32), norm_gain)
    hidden = jnp.concatenate([own_normed.astype(BF16), other_normed.astype(BF16)], axis=0)
    whole = jnp.zeros((2, 4, 4, 72, 1024), BF16)
    for step, block in ((0, near_line), (3, near_up), (1, near_down)):
        whole = put(whole, block[None, :, None], (core, 0, (z + step) & 3, 0, 0))
    for step, block in ((0, cross_line), (3, cross_up), (1, cross_down)):
        whole = put(whole, block[None, None], (1 - core, (x + step) & 3, 0, 0, 0))
    whole, hidden, near_far, cross_far = lax.optimization_barrier((whole, hidden, near_far, cross_far))
    whole = put(whole, near_far[None, :, None], (core, 0, (z + 2) & 3, 0, 0))
    whole = put(whole, cross_far[None, None], (1 - core, (x + 2) & 3, 0, 0, 0))
    full_qkv = whole.reshape(2304, 1024)

    groups = [[16 * y + i for i in range(16)] for y in range(2)]
    own_out = lax.all_gather(rows_out, "fsdp", axis=0, tiled=True, axis_index_groups=groups)
    other_out = send(own_out, CORE)
    full_out = jnp.concatenate([own_out, other_out], axis=0)

    flags = jnp.concatenate([near[72, :512].reshape(2, SEQ), cross[72, :512].reshape(2, SEQ)], axis=0)
    rows, cols = doc_numbers(flags)
    cosine, sine = rope_tables()

    packed = jnp.dot(hidden, full_qkv, preferred_element_type=F32)
    packed, upstream = lax.optimization_barrier((packed, upstream))
    heads, mixture = attention(packed, rows, cols, cosine, sine)
    own_mixture = jnp.concatenate([mixture[:512], send(mixture[512:], CORE)], axis=1)
    upstream = upstream.astype(F32)
    projected = jnp.dot(own_mixture, full_out, preferred_element_type=F32)

    post_back = jax.vjp(lambda values: normalize(values, post_gain), projected)[1]
    grad_proj = post_back(upstream)[0].astype(BF16)
    grad_mix = dot_nt(grad_proj, full_out).astype(BF16)
    grad_mix = jnp.concatenate([grad_mix[:, :512], send(grad_mix[:, 512:], CORE)], axis=0)
    both_proj = jnp.concatenate([grad_proj, send(grad_proj, CORE)], axis=0)
    partial_out = dot_tn(mixture, both_proj).astype(BF16).reshape(4, 4, 32, 2304)
    left = jnp.concatenate([partial_out[..., :1024], pack_rest(partial_out[..., 2048:])], axis=2)
    left, right = parts_of(left, 1, z), parts_of(partial_out[..., 1024:2048], 0, x)
    left_got, right_got = send_near(left, "z"), send_near(right, "x")
    grad_heads = attention_back(heads, after(grad_mix, *left, *right), rows, cols, cosine, sine)
    partial_qkv = dot_tn(hidden, grad_heads).astype(BF16).reshape(2, 4, 4, 72, 1024)
    near = [
        lax.dynamic_slice(partial_qkv, (core, 0, (z + d) & 3, 0, 0), (1, 4, 1, 72, 1024)).reshape(4, 72, 1024)
        for d in range(4)
    ]
    cross = [
        lax.dynamic_slice(partial_qkv, (1 - core, (x + d) & 3, 0, 0, 0), (1, 1, 4, 72, 1024)).reshape(4, 72, 1024)
        for d in range(4)
    ]
    near, cross, left_got, right_got = lax.optimization_barrier((near, cross, left_got, right_got))

    near_got, cross_got = send_near(near, "z"), send_near(cross, "x")
    grad_hidden = dot_nt(after(grad_heads, *near, *cross), full_qkv)
    grad_hidden = grad_hidden[:512] + send(grad_hidden[512:].astype(BF16), CORE).astype(F32)
    grad_rows = (upstream + pre_back(grad_hidden)[0]).astype(BF16)
    near, cross, left, right, near_got, cross_got, grad_rows = lax.optimization_barrier(
        (near, cross, left, right, near_got, cross_got, grad_rows)
    )
    grad_rows = send(grad_rows, TRADE_BACK)
    near_far, left_far = send(near[2], RING["z"][2]), send(left[2], RING["z"][2])
    cross_far, right_far = send(cross[2], RING["x"][2]), send(right[2], RING["x"][2])

    near_line = jnp.concatenate([total(near[0], *near_got, near_far), total(left[0], *left_got, left_far)], axis=1)
    cross_line = jnp.concatenate(
        [total(cross[0], *cross_got, cross_far), total(right[0], *right_got, right_far)], axis=1
    )
    sum_near = collect(parts_of(near_line, 0, x), "x")
    sum_cross = collect(parts_of(cross_line, 0, z), "z")
    sum_near, sum_cross, grad_rows = lax.optimization_barrier((sum_near, sum_cross, grad_rows))

    sum_near = send(jnp.concatenate([sum_near, sum_cross[72:]], axis=0), TRADE_BACK)
    sum_cross = send(sum_cross[:72], TRADE_CROSS)
    sum_out = jnp.concatenate([sum_near[72:104], sum_near[112:], unpack_rest(sum_near[104:112])], axis=1)
    sum_out = lax.optimization_barrier(sum_out).astype(F32)
    sum_near = sum_near[:72]
    sum_qkv = whole_columns(
        jnp.where(y_lo == 0, sum_near, sum_cross), jnp.where(y_lo == 0, sum_cross, sum_near)
    )
    sum_qkv = lax.optimization_barrier(sum_qkv).astype(F32)

    steps_done = float(SYNC_EVERY)
    inner_qkv, next_first_qkv, next_second_qkv = adam_step(
        part_qkv, sum_qkv / TOKENS, first_qkv[0], second_qkv[0], steps_done
    )
    inner_out, next_first_out, next_second_out = adam_step(
        part_out, sum_out / TOKENS, first_out[0], second_out[0], steps_done
    )
    change_qkv = (anchor_qkv - inner_qkv).astype(BF16)
    change_out = (anchor_out - inner_out).astype(BF16)
    change_rest = jnp.pad(pack_rest(change_out[:, 2048:]), ((0, 0), (0, 1024)))
    change = jnp.concatenate([change_qkv, change_out[:, :2048], change_rest], axis=0)
    pseudo = over_replicas(change)
    pseudo_qkv = pseudo[:72]
    pseudo_out = jnp.concatenate([pseudo[72:104], unpack_rest(pseudo[104:, :1024])], axis=1)
    outer_next_qkv = MOMENTUM * outer_qkv + pseudo_qkv
    outer_next_out = MOMENTUM * outer_out + pseudo_out
    anchor_next_qkv = anchor_qkv - OUTER_LR * (pseudo_qkv + MOMENTUM * outer_next_qkv)
    anchor_next_out = anchor_out - OUTER_LR * (pseudo_out + MOMENTUM * outer_next_out)
    return (
        grad_rows[None],
        next_first_qkv[None],
        next_first_out[None],
        next_second_qkv[None],
        next_second_out[None],
        anchor_next_qkv,
        anchor_next_out,
        outer_next_qkv,
        outer_next_out,
    )


def solution(mesh):
    rows = P("replica", "fsdp", None)
    shared = P("fsdp", None)
    in_specs = (rows, P("replica", "fsdp"), rows, P(), P(), rows, rows, shared, shared, rows, rows, rows, rows, shared, shared)
    out_specs = (rows, rows, rows, rows, rows, shared, shared, shared, shared)
    return jax.shard_map(per_device, mesh=mesh, in_specs=in_specs, out_specs=out_specs, check_vma=False)
```

```python
import functools

import jax
import jax.numpy as jnp
from jax import lax
from jax.experimental import pallas as pl
from jax.experimental.pallas import tpu as pltpu
from jax.sharding import PartitionSpec as P

HD = 256
SEQ = 256
SYNC_EVERY = 16
TOKENS = 16384

EPS_NORM = 1e-06
SOFTCAP = 50.0
ROPE_BASE = 10000.0
BETA_ONE = 0.9
BETA_TWO = 0.95
EPS_ADAM = 1e-08
INNER_LR = 0.001
DECAY = 0.1
OUTER_LR = 0.7
MOMENTUM = 0.9
START_ID = 2

BF16 = jnp.bfloat16
F32 = jnp.float32


def place(step):
    pairs = []
    for source in range(128):
        y_lo, x, z, y_hi, core = source // 64, source // 16 % 4, source // 4 % 4, source // 2 % 2, source % 2
        y_lo, x, z, y_hi, core = step(y_lo, x, z, y_hi, core)
        pairs.append((source, (((y_lo * 4 + x) * 4 + z) * 2 + y_hi) * 2 + core))
    return pairs


TRADE = place(lambda y, x, z, h, c: (1 - c, x, z, h, y))
TRADE_BACK = place(lambda y, x, z, h, c: (c, x, z, h, 1 - y))
TRADE_CROSS = place(lambda y, x, z, h, c: (1 - c, x, z, h, 1 - y))
CORE = place(lambda y, x, z, h, c: (y, x, z, h, 1 - c))
FAR = place(lambda y, x, z, h, c: (y, x, z, 1 - h, c))
RING = {
    "x": {d: place(lambda y, x, z, h, c, d=d: (y, (x + d) % 4, z, h, c)) for d in (1, 2, 3)},
    "z": {d: place(lambda y, x, z, h, c, d=d: (y, x, (z + d) % 4, h, c)) for d in (1, 2, 3)},
}


def send(values, pairs):
    return lax.ppermute(values, ("fsdp", "replica"), pairs)


def group_columns(values, group):
    return jnp.concatenate(
        [
            values[:, 512 * group : 512 * group + 512],
            values[:, 1024 + 256 * group : 1280 + 256 * group],
            values[:, 1536 + 256 * group : 1792 + 256 * group],
        ],
        axis=1,
    )


def whole_columns(first, second):
    return jnp.concatenate(
        [
            first[:, :512],
            second[:, :512],
            first[:, 512:768],
            second[:, 512:768],
            first[:, 768:],
            second[:, 768:],
        ],
        axis=1,
    )


def normalize(values, gain):
    return values * lax.rsqrt(jnp.mean(values * values, axis=-1, keepdims=True) + EPS_NORM) * gain


def rope_tables():
    freqs = ROPE_BASE ** (-2.0 * jnp.arange(HD // 2, dtype=F32) / HD)
    angles = jnp.arange(SEQ, dtype=F32)[:, None] * freqs[None, :]
    return jnp.cos(angles), jnp.sin(angles)


def doc_numbers(flags):
    ordered = (jnp.arange(SEQ)[:, None] <= jnp.arange(SEQ)[None, :]).astype(BF16)
    numbers = jnp.dot(flags, ordered, preferred_element_type=F32)
    return numbers[:, None, :], numbers[:, :, None]


def doc_mask(row_ref, col_ref):
    same_doc = col_ref[0] == row_ref[0]
    places = (SEQ, SEQ)
    causal = lax.broadcasted_iota(jnp.int32, places, 1) <= lax.broadcasted_iota(jnp.int32, places, 0)
    return same_doc & causal


def rotated(values, cosine, sine):
    first, second = values[:, : HD // 2], values[:, HD // 2 :]
    return jnp.concatenate(
        [first * cosine - second * sine, second * cosine + first * sine], axis=1
    ).astype(BF16)


def rotated_back(grads, cosine, sine):
    grads = grads.astype(BF16).astype(F32)
    first, second = grads[:, : HD // 2], grads[:, HD // 2 :]
    return jnp.concatenate(
        [first * cosine + second * sine, second * cosine - first * sine], axis=1
    ).astype(BF16)


def dot_nt(left, right):
    return lax.dot_general(left, right, (((1,), (1,)), ((), ())), preferred_element_type=F32)


def dot_tn(left, right):
    return lax.dot_general(left, right, (((0,), (0,)), ((), ())), preferred_element_type=F32)


def chance(query, key, mask):
    capped = jnp.tanh(dot_nt(query, key) * (HD**-0.5 / SOFTCAP))
    weights = jnp.where(mask, jnp.exp(SOFTCAP * capped), 0.0)
    return capped, weights / jnp.sum(weights, axis=1, keepdims=True)


def attention_kernel(packed_ref, row_ref, col_ref, cos_ref, sin_ref, heads_ref, mixture_ref):
    mask = doc_mask(row_ref, col_ref)
    cosine, sine = cos_ref[...], sin_ref[...]
    key = rotated(packed_ref[:, 512:768], cosine, sine)
    value = packed_ref[:, 768:].astype(BF16)
    heads_ref[:, 512:768] = key
    heads_ref[:, 768:] = value
    for head in range(2):
        columns = slice(head * HD, head * HD + HD)
        query = rotated(packed_ref[:, columns], cosine, sine)
        heads_ref[:, columns] = query
        chances = chance(query, key, mask)[1].astype(BF16)
        mixture_ref[:, columns] = jnp.dot(chances, value, preferred_element_type=F32).astype(BF16)


def attention_back_kernel(heads_ref, grad_ref, row_ref, col_ref, cos_ref, sin_ref, out_ref):
    mask = doc_mask(row_ref, col_ref)
    cosine, sine = cos_ref[...], sin_ref[...]
    key, value = heads_ref[:, 512:768], heads_ref[:, 768:]
    grad_key = jnp.zeros((SEQ, HD), F32)
    grad_value = jnp.zeros((SEQ, HD), F32)
    for head in range(2):
        columns = slice(head * HD, head * HD + HD)
        query, grad = heads_ref[:, columns], grad_ref[:, columns]
        capped, chances = chance(query, key, mask)
        grad_chance = dot_nt(grad, value).astype(BF16).astype(F32)
        inner = jnp.sum(grad_chance * chances, axis=1, keepdims=True)
        grad_score = chances * (grad_chance - inner) * (1.0 - capped * capped) * HD**-0.5
        grad_score = grad_score.astype(BF16)
        grad_query = jnp.dot(grad_score, key, preferred_element_type=F32)
        out_ref[:, columns] = rotated_back(grad_query, cosine, sine)
        grad_key += dot_tn(grad_score, query)
        grad_value += dot_tn(chances.astype(BF16), grad)
    out_ref[:, 512:768] = rotated_back(grad_key, cosine, sine)
    out_ref[:, 768:] = grad_value.astype(BF16)


def per_sequence(width):
    return pl.BlockSpec((SEQ, width), lambda s: (s, 0))


DOC_SPECS = [
    pl.BlockSpec((1, 1, SEQ), lambda s: (s, 0, 0)),
    pl.BlockSpec((1, SEQ, 1), lambda s: (s, 0, 0)),
    pl.BlockSpec((SEQ, HD // 2), lambda s: (0, 0)),
    pl.BlockSpec((SEQ, HD // 2), lambda s: (0, 0)),
]
KERNEL_PARAMS = pltpu.CompilerParams(vmem_limit_bytes=12 * 1024 * 1024)


def attention(packed, rows, cols, cosine, sine):
    count = packed.shape[0]
    return pl.pallas_call(
        attention_kernel,
        grid=(count // SEQ,),
        in_specs=[per_sequence(1024)] + DOC_SPECS,
        out_specs=[per_sequence(1024), per_sequence(512)],
        out_shape=[jax.ShapeDtypeStruct((count, 1024), BF16), jax.ShapeDtypeStruct((count, 512), BF16)],
        compiler_params=KERNEL_PARAMS,
        cost_estimate=pl.CostEstimate(flops=6 * count * 1024 * SEQ, bytes_accessed=8 * count * 1024, transcendentals=4 * count * SEQ),
        name="attention",
    )(packed, rows, cols, cosine, sine)


def attention_back(heads, grads, rows, cols, cosine, sine):
    count = heads.shape[0]
    return pl.pallas_call(
        attention_back_kernel,
        grid=(count // SEQ,),
        in_specs=[per_sequence(1024), per_sequence(512)] + DOC_SPECS,
        out_specs=per_sequence(1024),
        out_shape=jax.ShapeDtypeStruct((count, 1024), BF16),
        compiler_params=KERNEL_PARAMS,
        cost_estimate=pl.CostEstimate(flops=12 * count * 1024 * SEQ, bytes_accessed=8 * count * 1024, transcendentals=4 * count * SEQ),
        name="attention_back",
    )(heads, grads, rows, cols, cosine, sine)


def norm_kernel(own_ref, other_ref, gain_ref, out_ref):
    step = pl.program_id(0)

    @pl.when(step < 2)
    def _():
        out_ref[...] = normalize(own_ref[...].astype(F32), gain_ref[...]).astype(BF16)

    @pl.when(step >= 2)
    def _():
        out_ref[...] = normalize(other_ref[...].astype(F32), gain_ref[...]).astype(BF16)


def norm_rows(own, other, gain):
    width = own.shape[1]
    return pl.pallas_call(
        norm_kernel,
        grid=(4,),
        in_specs=[
            pl.BlockSpec((256, width), lambda s: (jnp.minimum(s, 1), 0)),
            pl.BlockSpec((256, width), lambda s: (jnp.maximum(s - 2, 0), 0)),
            pl.BlockSpec((1, width), lambda s: (0, 0)),
        ],
        out_specs=pl.BlockSpec((256, width), lambda s: (s, 0)),
        out_shape=jax.ShapeDtypeStruct((1024, width), BF16),
        compiler_params=pltpu.CompilerParams(vmem_limit_bytes=16 * 1024 * 1024),
        name="norm_rows",
    )(own, other, gain[None])


def input_grad_kernel(own_ref, other_ref, near_ref, far_ref, tokens_ref, upstream_ref, gain_ref, out_ref, grad_ref):
    step = pl.program_id(0)
    columns = pl.ds(pl.multiple_of(step * 256, 256), 256)
    grad_ref[:, columns] = dot_nt(own_ref[...], near_ref[...]) + dot_nt(other_ref[...], far_ref[...])

    @pl.when(step == 8)
    def _():
        def rows_back(i, carry):
            rows = pl.ds(pl.multiple_of(i * 64, 64), 64)
            values = tokens_ref[rows, :].astype(F32)
            grads = grad_ref[rows, :] * gain_ref[...]
            scale = lax.rsqrt(jnp.mean(values * values, axis=-1, keepdims=True) + EPS_NORM)
            inner = jnp.mean(grads * values, axis=-1, keepdims=True) * scale * scale * scale
            total_grad = upstream_ref[rows, :].astype(F32) + (grads * scale - values * inner)
            out_ref[rows, :] = total_grad.astype(BF16)
            return carry

        lax.fori_loop(0, 8, rows_back, 0)


def input_grad(heads, other_heads, own_qkv, other_qkv, tokens, upstream, gain):
    count, width = tokens.shape

    def whole(shape):
        return pl.BlockSpec(shape, lambda s: (0, 0))

    return pl.pallas_call(
        input_grad_kernel,
        grid=(width // 256,),
        in_specs=[
            whole((count, 1024)),
            whole((count, 1024)),
            pl.BlockSpec((256, 1024), lambda s: (s, 0)),
            pl.BlockSpec((256, 1024), lambda s: (s, 0)),
            whole((count, width)),
            whole((count, width)),
            whole((1, width)),
        ],
        out_specs=whole((count, width)),
        out_shape=jax.ShapeDtypeStruct((count, width), BF16),
        scratch_shapes=[pltpu.VMEM((count, width), F32)],
        compiler_params=pltpu.CompilerParams(vmem_limit_bytes=40 * 1024 * 1024),
        name="input_grad",
    )(heads, other_heads, own_qkv, other_qkv, tokens, upstream, gain[None])


def after(values, *others):
    return lax.optimization_barrier((values, *others))[0]


def parts_of(values, axis, index):
    return [lax.dynamic_index_in_dim(values, (index + d) & 3, axis, keepdims=False) for d in range(4)]


def put(whole, block, start):
    return lax.dynamic_update_slice(whole, block, start)


def line_of(block, axis, index):
    line = jnp.zeros((4,) + block.shape, BF16)
    line = put(line, block[None], (index, 0, 0))
    ahead, behind = both_ways(block, axis)
    across = send(ahead, RING[axis][1])
    for step, received in ((3, ahead), (1, behind), (2, across)):
        line = put(line, received[None], ((index + step) & 3, 0, 0))
    return line


def both_ways(line, axis):
    return send(line, RING[axis][1]), send(line, RING[axis][3])


def first_round(parts, axis, way):
    return send(parts[2], RING[axis][way]), send(parts[4 - way], RING[axis][4 - way])


def second_round(parts, got, axis, way):
    return send(add(parts[way], got[0]), RING[axis][way])


def pack_rest(rest):
    return jnp.concatenate([rest[..., 8 * k : 8 * k + 8, :] for k in range(4)], axis=-1)


def unpack_rest(rest):
    return jnp.concatenate([rest[:, 256 * k : 256 * k + 256] for k in range(4)], axis=0)


def add(left, right):
    return (left.astype(F32) + right.astype(F32)).astype(BF16)


def total(*terms):
    return functools.reduce(lambda left, right: left + right, [term.astype(F32) for term in terms]).astype(BF16)


def collect(parts, axis):
    return total(parts[0], *[send(parts[step], RING[axis][step]) for step in (1, 3, 2)])


def adam_step(weights, grads, first, second, steps_done):
    first_next = BETA_ONE * first + (1.0 - BETA_ONE) * grads
    second_next = BETA_TWO * second + (1.0 - BETA_TWO) * grads * grads
    first_hat = first_next / (1.0 - BETA_ONE**steps_done)
    second_hat = second_next / (1.0 - BETA_TWO**steps_done)
    master = weights.astype(F32)
    inner = master - INNER_LR * (first_hat / (jnp.sqrt(second_hat) + EPS_ADAM) + DECAY * master)
    return (inner, first_next, second_next)


def over_replicas(change):
    pair = add(change, send(change, CORE))
    return (pair.astype(F32) + send(pair, FAR).astype(F32)) / 4.0


def per_device(
    tokens,
    token_ids,
    cotangent,
    norm_gain,
    post_gain,
    local_qkv,
    local_out,
    anchor_qkv,
    anchor_out,
    first_qkv,
    first_out,
    second_qkv,
    second_out,
    outer_qkv,
    outer_out,
):
    place_fsdp = lax.axis_index("fsdp")
    y_lo, x, z = place_fsdp >> 4, (place_fsdp >> 2) & 3, place_fsdp & 3
    core = lax.axis_index("replica") & 1
    part_qkv, part_out = local_qkv[0], local_out[0]

    flags = (token_ids[0] == START_ID).astype(BF16).reshape(1, 512)
    flags = jnp.pad(flags, ((0, 7), (0, 512)))
    group_a, group_b = group_columns(part_qkv, 0), group_columns(part_qkv, 1)
    near = send(jnp.concatenate([jnp.where(y_lo == 0, group_a, group_b), flags], axis=0), TRADE)
    cross = send(jnp.concatenate([jnp.where(y_lo == 0, group_b, group_a), flags], axis=0), TRADE_CROSS)
    rows_out = send(part_out, TRADE)
    near, cross, rows_out = lax.optimization_barrier((near, cross, rows_out))

    tokens_a = send(after(tokens[0, :256], near), TRADE)
    near_line = line_of(near[:72], "x", x)
    cross_line = line_of(cross[:72], "z", z)
    near_line, cross_line, tokens_a = lax.optimization_barrier((near_line, cross_line, tokens_a))

    tokens_b = send(after(tokens[0, 256:], tokens_a), TRADE)
    near_up, near_down = both_ways(near_line, "z")
    cross_up, cross_down = both_ways(cross_line, "x")
    own_tokens = jnp.concatenate([tokens_a, tokens_b], axis=0)
    groups = [[16 * y + i for i in range(16)] for y in range(2)]
    own_out = lax.all_gather(rows_out, "fsdp", axis=0, tiled=True, axis_index_groups=groups)
    near_line, cross_line, near_up, near_down, cross_up, cross_down, own_tokens, own_out = lax.optimization_barrier(
        (near_line, cross_line, near_up, near_down, cross_up, cross_down, own_tokens, own_out)
    )

    near_far = send(near_up, RING["z"][1])
    cross_far = send(cross_up, RING["x"][1])
    other_tokens = send(own_tokens, CORE)
    upstream = send(after(cotangent[0], own_tokens), TRADE)
    hidden = norm_rows(own_tokens, other_tokens, norm_gain)
    whole = jnp.zeros((2, 4, 4, 72, 1024), BF16)
    for step, block in ((0, near_line), (3, near_up), (1, near_down)):
        whole = put(whole, block[None, :, None], (core, 0, (z + step) & 3, 0, 0))
    for step, block in ((0, cross_line), (3, cross_up), (1, cross_down)):
        whole = put(whole, block[None, None], (1 - core, (x + step) & 3, 0, 0, 0))
    whole, hidden, near_far, cross_far = lax.optimization_barrier((whole, hidden, near_far, cross_far))
    other_out = send(own_out, CORE)
    whole = put(whole, near_far[None, :, None], (core, 0, (z + 2) & 3, 0, 0))
    whole = put(whole, cross_far[None, None], (1 - core, (x + 2) & 3, 0, 0, 0))
    full_qkv = whole.reshape(2304, 1024)
    other_qkv = send(full_qkv, CORE)

    flags = jnp.concatenate([near[72, :512].reshape(2, SEQ), cross[72, :512].reshape(2, SEQ)], axis=0)
    rows, cols = doc_numbers(flags)
    cosine, sine = rope_tables()

    packed = jnp.dot(hidden, full_qkv, preferred_element_type=F32)
    heads, mixture = attention(packed, rows, cols, cosine, sine)
    other_mixture = send(mixture[512:], CORE)
    other_mixture, upstream = lax.optimization_barrier((other_mixture, upstream))
    projected = jnp.dot(mixture[:512], own_out, preferred_element_type=F32)
    projected = projected + jnp.dot(other_mixture, other_out, preferred_element_type=F32)

    post_back = jax.vjp(lambda values: normalize(values, post_gain), projected)[1]
    grad_proj = post_back(upstream.astype(F32))[0].astype(BF16)
    other_mix = send(dot_nt(grad_proj, other_out).astype(BF16), CORE)
    grad_mix = jnp.concatenate([dot_nt(grad_proj, own_out).astype(BF16), other_mix], axis=0)
    both_proj = jnp.concatenate([grad_proj, send(grad_proj, CORE)], axis=0)
    partial_out = dot_tn(mixture, both_proj).astype(BF16).reshape(4, 4, 32, 2304)
    left = jnp.concatenate([partial_out[..., :1024], pack_rest(partial_out[..., 2048:])], axis=2)
    left, right = parts_of(left, 1, z), parts_of(partial_out[..., 1024:2048], 0, x)
    left_got, right_got = first_round(left, "z", 3), first_round(right, "x", 3)
    grad_mix, other_qkv = lax.optimization_barrier((grad_mix, other_qkv, *left, *right))[:2]
    grad_heads = attention_back(heads, grad_mix, rows, cols, cosine, sine)
    other_heads = send(grad_heads[512:], CORE)
    partial_qkv = dot_tn(hidden, grad_heads).astype(BF16).reshape(2, 4, 4, 72, 1024)
    near = [
        lax.dynamic_slice(partial_qkv, (core, 0, (z + d) & 3, 0, 0), (1, 4, 1, 72, 1024)).reshape(4, 72, 1024)
        for d in range(4)
    ]
    cross = [
        lax.dynamic_slice(partial_qkv, (1 - core, (x + d) & 3, 0, 0, 0), (1, 1, 4, 72, 1024)).reshape(4, 72, 1024)
        for d in range(4)
    ]
    near, cross, left_got, right_got, other_heads = lax.optimization_barrier(
        (near, cross, left_got, right_got, other_heads)
    )

    near_got, cross_got = first_round(near, "z", 1), first_round(cross, "x", 1)
    grad_rows = input_grad(
        after(grad_heads, *near, *cross), other_heads, full_qkv, other_qkv, own_tokens, upstream, norm_gain
    )
    near, cross, left, right, near_got, cross_got, grad_rows = lax.optimization_barrier(
        (near, cross, left, right, near_got, cross_got, grad_rows)
    )
    grad_rows = send(grad_rows, TRADE_BACK)
    near_far, left_far = second_round(near, near_got, "z", 1), second_round(left, left_got, "z", 3)
    cross_far, right_far = second_round(cross, cross_got, "x", 1), second_round(right, right_got, "x", 3)

    near_line = jnp.concatenate([total(near[0], near_got[1], near_far), total(left[0], left_got[1], left_far)], axis=1)
    cross_line = jnp.concatenate(
        [total(cross[0], cross_got[1], cross_far), total(right[0], right_got[1], right_far)], axis=1
    )
    sum_near = collect(parts_of(near_line, 0, x), "x")
    sum_cross = collect(parts_of(cross_line, 0, z), "z")
    sum_near, sum_cross, grad_rows = lax.optimization_barrier((sum_near, sum_cross, grad_rows))

    sum_near = send(jnp.concatenate([sum_near, sum_cross[72:]], axis=0), TRADE_BACK)
    sum_cross = send(sum_cross[:72], TRADE_CROSS)
    sum_out = jnp.concatenate([sum_near[72:104], sum_near[112:], unpack_rest(sum_near[104:112])], axis=1)
    sum_out = lax.optimization_barrier(sum_out).astype(F32)
    sum_near = sum_near[:72]
    sum_qkv = whole_columns(
        jnp.where(y_lo == 0, sum_near, sum_cross), jnp.where(y_lo == 0, sum_cross, sum_near)
    )
    sum_qkv = lax.optimization_barrier(sum_qkv).astype(F32)

    steps_done = float(SYNC_EVERY)
    inner_qkv, next_first_qkv, next_second_qkv = adam_step(
        part_qkv, sum_qkv / TOKENS, first_qkv[0], second_qkv[0], steps_done
    )
    inner_out, next_first_out, next_second_out = adam_step(
        part_out, sum_out / TOKENS, first_out[0], second_out[0], steps_done
    )
    change_qkv = (anchor_qkv - inner_qkv).astype(BF16)
    change_out = (anchor_out - inner_out).astype(BF16)
    change_rest = jnp.pad(pack_rest(change_out[:, 2048:]), ((0, 0), (0, 1024)))
    change = jnp.concatenate([change_qkv, change_out[:, :2048], change_rest], axis=0)
    pseudo = over_replicas(change)
    pseudo_qkv = pseudo[:72]
    pseudo_out = jnp.concatenate([pseudo[72:104], unpack_rest(pseudo[104:, :1024])], axis=1)
    outer_next_qkv = MOMENTUM * outer_qkv + pseudo_qkv
    outer_next_out = MOMENTUM * outer_out + pseudo_out
    anchor_next_qkv = anchor_qkv - OUTER_LR * (pseudo_qkv + MOMENTUM * outer_next_qkv)
    anchor_next_out = anchor_out - OUTER_LR * (pseudo_out + MOMENTUM * outer_next_out)
    return (
        grad_rows[None],
        next_first_qkv[None],
        next_first_out[None],
        next_second_qkv[None],
        next_second_out[None],
        anchor_next_qkv,
        anchor_next_out,
        outer_next_qkv,
        outer_next_out,
    )


def solution(mesh):
    rows = P("replica", "fsdp", None)
    shared = P("fsdp", None)
    in_specs = (rows, P("replica", "fsdp"), rows, P(), P(), rows, rows, shared, shared, rows, rows, rows, rows, shared, shared)
    out_specs = (rows, rows, rows, rows, rows, shared, shared, shared, shared)
    return jax.shard_map(per_device, mesh=mesh, in_specs=in_specs, out_specs=out_specs, check_vma=False)
```

```python
import functools

import jax
import jax.numpy as jnp
from jax import lax
from jax.experimental import pallas as pl
from jax.experimental.pallas import tpu as pltpu
from jax.sharding import PartitionSpec as P

HD = 256
SEQ = 256
SYNC_EVERY = 16
TOKENS = 16384

EPS_NORM = 1e-06
SOFTCAP = 50.0
ROPE_BASE = 10000.0
BETA_ONE = 0.9
BETA_TWO = 0.95
EPS_ADAM = 1e-08
INNER_LR = 0.001
DECAY = 0.1
OUTER_LR = 0.7
MOMENTUM = 0.9
START_ID = 2

BF16 = jnp.bfloat16
F32 = jnp.float32


def place(step):
    pairs = []
    for source in range(128):
        y_lo, x, z, y_hi, core = source // 64, source // 16 % 4, source // 4 % 4, source // 2 % 2, source % 2
        y_lo, x, z, y_hi, core = step(y_lo, x, z, y_hi, core)
        pairs.append((source, (((y_lo * 4 + x) * 4 + z) * 2 + y_hi) * 2 + core))
    return pairs


TRADE = place(lambda y, x, z, h, c: (1 - c, x, z, h, y))
TRADE_BACK = place(lambda y, x, z, h, c: (c, x, z, h, 1 - y))
TRADE_CROSS = place(lambda y, x, z, h, c: (1 - c, x, z, h, 1 - y))
CORE = place(lambda y, x, z, h, c: (y, x, z, h, 1 - c))
FAR = place(lambda y, x, z, h, c: (y, x, z, 1 - h, c))
RING = {
    "x": {d: place(lambda y, x, z, h, c, d=d: (y, (x + d) % 4, z, h, c)) for d in (1, 2, 3)},
    "z": {d: place(lambda y, x, z, h, c, d=d: (y, x, (z + d) % 4, h, c)) for d in (1, 2, 3)},
}


def send(values, pairs):
    return lax.ppermute(values, ("fsdp", "replica"), pairs)


def group_columns(values, group):
    return jnp.concatenate(
        [
            values[:, 512 * group : 512 * group + 512],
            values[:, 1024 + 256 * group : 1280 + 256 * group],
            values[:, 1536 + 256 * group : 1792 + 256 * group],
        ],
        axis=1,
    )


def whole_columns(first, second):
    return jnp.concatenate(
        [
            first[:, :512],
            second[:, :512],
            first[:, 512:768],
            second[:, 512:768],
            first[:, 768:],
            second[:, 768:],
        ],
        axis=1,
    )


def normalize(values, gain):
    return values * lax.rsqrt(jnp.mean(values * values, axis=-1, keepdims=True) + EPS_NORM) * gain


def rope_tables():
    freqs = ROPE_BASE ** (-2.0 * jnp.arange(HD // 2, dtype=F32) / HD)
    angles = jnp.arange(SEQ, dtype=F32)[:, None] * freqs[None, :]
    return jnp.cos(angles), jnp.sin(angles)


def doc_numbers(flags):
    ordered = (jnp.arange(SEQ)[:, None] <= jnp.arange(SEQ)[None, :]).astype(BF16)
    numbers = jnp.dot(flags, ordered, preferred_element_type=F32)
    return numbers[:, None, :], numbers[:, :, None]


def doc_mask(row_ref, col_ref):
    same_doc = col_ref[0] == row_ref[0]
    places = (SEQ, SEQ)
    causal = lax.broadcasted_iota(jnp.int32, places, 1) <= lax.broadcasted_iota(jnp.int32, places, 0)
    return same_doc & causal


def rotated(values, cosine, sine):
    first, second = values[:, : HD // 2], values[:, HD // 2 :]
    return jnp.concatenate(
        [first * cosine - second * sine, second * cosine + first * sine], axis=1
    ).astype(BF16)


def rotated_back(grads, cosine, sine):
    grads = grads.astype(BF16).astype(F32)
    first, second = grads[:, : HD // 2], grads[:, HD // 2 :]
    return jnp.concatenate(
        [first * cosine + second * sine, second * cosine - first * sine], axis=1
    ).astype(BF16)


def dot_nt(left, right):
    return lax.dot_general(left, right, (((1,), (1,)), ((), ())), preferred_element_type=F32)


def dot_tn(left, right):
    return lax.dot_general(left, right, (((0,), (0,)), ((), ())), preferred_element_type=F32)


def chance(query, key, mask):
    capped = jnp.tanh(dot_nt(query, key) * (HD**-0.5 / SOFTCAP))
    weights = jnp.where(mask, jnp.exp(SOFTCAP * capped), 0.0)
    return capped, weights / jnp.sum(weights, axis=1, keepdims=True)


def attention_kernel(packed_ref, row_ref, col_ref, cos_ref, sin_ref, heads_ref, mixture_ref):
    mask = doc_mask(row_ref, col_ref)
    cosine, sine = cos_ref[...], sin_ref[...]
    key = rotated(packed_ref[:, 512:768], cosine, sine)
    value = packed_ref[:, 768:].astype(BF16)
    heads_ref[:, 512:768] = key
    heads_ref[:, 768:] = value
    for head in range(2):
        columns = slice(head * HD, head * HD + HD)
        query = rotated(packed_ref[:, columns], cosine, sine)
        heads_ref[:, columns] = query
        chances = chance(query, key, mask)[1].astype(BF16)
        mixture_ref[:, columns] = jnp.dot(chances, value, preferred_element_type=F32).astype(BF16)


def attention_back_kernel(heads_ref, grad_ref, row_ref, col_ref, cos_ref, sin_ref, out_ref):
    mask = doc_mask(row_ref, col_ref)
    cosine, sine = cos_ref[...], sin_ref[...]
    key, value = heads_ref[:, 512:768], heads_ref[:, 768:]
    grad_key = jnp.zeros((SEQ, HD), F32)
    grad_value = jnp.zeros((SEQ, HD), F32)
    for head in range(2):
        columns = slice(head * HD, head * HD + HD)
        query, grad = heads_ref[:, columns], grad_ref[:, columns]
        capped, chances = chance(query, key, mask)
        grad_chance = dot_nt(grad, value).astype(BF16).astype(F32)
        inner = jnp.sum(grad_chance * chances, axis=1, keepdims=True)
        grad_score = chances * (grad_chance - inner) * (1.0 - capped * capped) * HD**-0.5
        grad_score = grad_score.astype(BF16)
        grad_query = jnp.dot(grad_score, key, preferred_element_type=F32)
        out_ref[:, columns] = rotated_back(grad_query, cosine, sine)
        grad_key += dot_tn(grad_score, query)
        grad_value += dot_tn(chances.astype(BF16), grad)
    out_ref[:, 512:768] = rotated_back(grad_key, cosine, sine)
    out_ref[:, 768:] = grad_value.astype(BF16)


def per_sequence(width):
    return pl.BlockSpec((SEQ, width), lambda s: (s, 0))


DOC_SPECS = [
    pl.BlockSpec((1, 1, SEQ), lambda s: (s, 0, 0)),
    pl.BlockSpec((1, SEQ, 1), lambda s: (s, 0, 0)),
    pl.BlockSpec((SEQ, HD // 2), lambda s: (0, 0)),
    pl.BlockSpec((SEQ, HD // 2), lambda s: (0, 0)),
]
KERNEL_PARAMS = pltpu.CompilerParams(vmem_limit_bytes=12 * 1024 * 1024)


def attention(packed, rows, cols, cosine, sine):
    count = packed.shape[0]
    return pl.pallas_call(
        attention_kernel,
        grid=(count // SEQ,),
        in_specs=[per_sequence(1024)] + DOC_SPECS,
        out_specs=[per_sequence(1024), per_sequence(512)],
        out_shape=[jax.ShapeDtypeStruct((count, 1024), BF16), jax.ShapeDtypeStruct((count, 512), BF16)],
        compiler_params=KERNEL_PARAMS,
        cost_estimate=pl.CostEstimate(flops=6 * count * 1024 * SEQ, bytes_accessed=8 * count * 1024, transcendentals=4 * count * SEQ),
        name="attention",
    )(packed, rows, cols, cosine, sine)


def attention_back(heads, grads, rows, cols, cosine, sine):
    count = heads.shape[0]
    return pl.pallas_call(
        attention_back_kernel,
        grid=(count // SEQ,),
        in_specs=[per_sequence(1024), per_sequence(512)] + DOC_SPECS,
        out_specs=per_sequence(1024),
        out_shape=jax.ShapeDtypeStruct((count, 1024), BF16),
        compiler_params=KERNEL_PARAMS,
        cost_estimate=pl.CostEstimate(flops=12 * count * 1024 * SEQ, bytes_accessed=8 * count * 1024, transcendentals=4 * count * SEQ),
        name="attention_back",
    )(heads, grads, rows, cols, cosine, sine)


def norm_kernel(own_ref, other_ref, gain_ref, out_ref):
    step = pl.program_id(0)

    @pl.when(step < 2)
    def _():
        out_ref[...] = normalize(own_ref[...].astype(F32), gain_ref[...]).astype(BF16)

    @pl.when(step >= 2)
    def _():
        out_ref[...] = normalize(other_ref[...].astype(F32), gain_ref[...]).astype(BF16)


def norm_rows(own, other, gain):
    width = own.shape[1]
    return pl.pallas_call(
        norm_kernel,
        grid=(4,),
        in_specs=[
            pl.BlockSpec((256, width), lambda s: (jnp.minimum(s, 1), 0)),
            pl.BlockSpec((256, width), lambda s: (jnp.maximum(s - 2, 0), 0)),
            pl.BlockSpec((1, width), lambda s: (0, 0)),
        ],
        out_specs=pl.BlockSpec((256, width), lambda s: (s, 0)),
        out_shape=jax.ShapeDtypeStruct((1024, width), BF16),
        compiler_params=pltpu.CompilerParams(vmem_limit_bytes=16 * 1024 * 1024),
        name="norm_rows",
    )(own, other, gain[None])


def input_grad_kernel(own_ref, other_ref, near_ref, far_ref, tokens_ref, upstream_ref, gain_ref, out_ref, grad_ref):
    step = pl.program_id(0)
    columns = pl.ds(pl.multiple_of(step * 256, 256), 256)
    grad_ref[:, columns] = dot_nt(own_ref[...], near_ref[...]) + dot_nt(other_ref[...], far_ref[...])

    @pl.when(step == 8)
    def _():
        def rows_back(i, carry):
            rows = pl.ds(pl.multiple_of(i * 64, 64), 64)
            values = tokens_ref[rows, :].astype(F32)
            grads = grad_ref[rows, :] * gain_ref[...]
            scale = lax.rsqrt(jnp.mean(values * values, axis=-1, keepdims=True) + EPS_NORM)
            inner = jnp.mean(grads * values, axis=-1, keepdims=True) * scale * scale * scale
            total_grad = upstream_ref[rows, :].astype(F32) + (grads * scale - values * inner)
            out_ref[rows, :] = total_grad.astype(BF16)
            return carry

        lax.fori_loop(0, 8, rows_back, 0)


def input_grad(heads, other_heads, own_qkv, other_qkv, tokens, upstream, gain):
    count, width = tokens.shape

    def whole(shape):
        return pl.BlockSpec(shape, lambda s: (0, 0))

    return pl.pallas_call(
        input_grad_kernel,
        grid=(width // 256,),
        in_specs=[
            whole((count, 1024)),
            whole((count, 1024)),
            pl.BlockSpec((256, 1024), lambda s: (s, 0)),
            pl.BlockSpec((256, 1024), lambda s: (s, 0)),
            whole((count, width)),
            whole((count, width)),
            whole((1, width)),
        ],
        out_specs=whole((count, width)),
        out_shape=jax.ShapeDtypeStruct((count, width), BF16),
        scratch_shapes=[pltpu.VMEM((count, width), F32)],
        compiler_params=pltpu.CompilerParams(vmem_limit_bytes=40 * 1024 * 1024),
        name="input_grad",
    )(heads, other_heads, own_qkv, other_qkv, tokens, upstream, gain[None])


def after(values, *others):
    return lax.optimization_barrier((values, *others))[0]


def parts_of(values, axis, index):
    return [lax.dynamic_index_in_dim(values, (index + d) & 3, axis, keepdims=False) for d in range(4)]


def put(whole, block, start):
    return lax.dynamic_update_slice(whole, block, start)


def line_of(block, axis, index):
    line = jnp.zeros((4,) + block.shape, BF16)
    line = put(line, block[None], (index, 0, 0))
    ahead, behind = both_ways(block, axis)
    across = send(ahead, RING[axis][1])
    for step, received in ((3, ahead), (1, behind), (2, across)):
        line = put(line, received[None], ((index + step) & 3, 0, 0))
    return line


def both_ways(line, axis):
    return send(line, RING[axis][1]), send(line, RING[axis][3])


def first_round(parts, axis, way):
    return send(parts[2], RING[axis][way]), send(parts[4 - way], RING[axis][4 - way])


def second_round(parts, got, axis, way):
    return send(add(parts[way], got[0]), RING[axis][way])


def pack_rest(rest):
    return jnp.concatenate([rest[..., 8 * k : 8 * k + 8, :] for k in range(4)], axis=-1)


def unpack_rest(rest):
    return jnp.concatenate([rest[:, 256 * k : 256 * k + 256] for k in range(4)], axis=0)


def add(left, right):
    return (left.astype(F32) + right.astype(F32)).astype(BF16)


def total(*terms):
    return functools.reduce(lambda left, right: left + right, [term.astype(F32) for term in terms]).astype(BF16)


def collect(parts, axis):
    got = first_round(parts, axis, 1)
    return total(parts[0], got[1], second_round(parts, got, axis, 1))


def adam_step(weights, grads, first, second, steps_done):
    first_next = BETA_ONE * first + (1.0 - BETA_ONE) * grads
    second_next = BETA_TWO * second + (1.0 - BETA_TWO) * grads * grads
    first_hat = first_next / (1.0 - BETA_ONE**steps_done)
    second_hat = second_next / (1.0 - BETA_TWO**steps_done)
    master = weights.astype(F32)
    inner = master - INNER_LR * (first_hat / (jnp.sqrt(second_hat) + EPS_ADAM) + DECAY * master)
    return (inner, first_next, second_next)


def over_replicas(change):
    pair = add(change, send(change, CORE))
    return (pair.astype(F32) + send(pair, FAR).astype(F32)) / 4.0


def per_device(
    tokens,
    token_ids,
    cotangent,
    norm_gain,
    post_gain,
    local_qkv,
    local_out,
    anchor_qkv,
    anchor_out,
    first_qkv,
    first_out,
    second_qkv,
    second_out,
    outer_qkv,
    outer_out,
):
    place_fsdp = lax.axis_index("fsdp")
    y_lo, x, z = place_fsdp >> 4, (place_fsdp >> 2) & 3, place_fsdp & 3
    core = lax.axis_index("replica") & 1
    part_qkv, part_out = local_qkv[0], local_out[0]

    flags = (token_ids[0] == START_ID).astype(BF16).reshape(1, 512)
    flags = jnp.pad(flags, ((0, 7), (0, 512)))
    group_a, group_b = group_columns(part_qkv, 0), group_columns(part_qkv, 1)
    near = send(jnp.concatenate([jnp.where(y_lo == 0, group_a, group_b), flags], axis=0), TRADE)
    cross = send(jnp.concatenate([jnp.where(y_lo == 0, group_b, group_a), flags], axis=0), TRADE_CROSS)
    rows_out = send(part_out, TRADE)
    tokens_a, tokens_b = tokens[0, :192], tokens[0, 192:]
    near, cross, rows_out, tokens_a, tokens_b = lax.optimization_barrier(
        (near, cross, rows_out, tokens_a, tokens_b)
    )

    tokens_a = send(tokens_a, TRADE)
    near_line = line_of(near[:72], "x", x)
    cross_line = line_of(cross[:72], "z", z)
    near_line, cross_line, tokens_a = lax.optimization_barrier((near_line, cross_line, tokens_a))

    tokens_b = send(after(tokens_b, tokens_a), TRADE)
    near_up, near_down = both_ways(near_line, "z")
    cross_up, cross_down = both_ways(cross_line, "x")
    own_tokens = jnp.concatenate([tokens_a, tokens_b], axis=0)
    groups = [[16 * y + i for i in range(16)] for y in range(2)]
    own_out = lax.all_gather(rows_out, "fsdp", axis=0, tiled=True, axis_index_groups=groups)
    near_line, cross_line, near_up, near_down, cross_up, cross_down, own_tokens, own_out = lax.optimization_barrier(
        (near_line, cross_line, near_up, near_down, cross_up, cross_down, own_tokens, own_out)
    )

    near_far = send(near_up, RING["z"][1])
    cross_far = send(cross_up, RING["x"][1])
    other_tokens = send(own_tokens, CORE)
    upstream = send(after(cotangent[0], own_tokens), TRADE)
    hidden = norm_rows(own_tokens, other_tokens, norm_gain)
    whole = jnp.zeros((2, 4, 4, 72, 1024), BF16)
    for step, block in ((0, near_line), (3, near_up), (1, near_down)):
        whole = put(whole, block[None, :, None], (core, 0, (z + step) & 3, 0, 0))
    for step, block in ((0, cross_line), (3, cross_up), (1, cross_down)):
        whole = put(whole, block[None, None], (1 - core, (x + step) & 3, 0, 0, 0))
    whole, hidden, near_far, cross_far = lax.optimization_barrier((whole, hidden, near_far, cross_far))
    other_out = send(own_out, CORE)
    whole = put(whole, near_far[None, :, None], (core, 0, (z + 2) & 3, 0, 0))
    whole = put(whole, cross_far[None, None], (1 - core, (x + 2) & 3, 0, 0, 0))
    full_qkv = whole.reshape(2304, 1024)
    other_qkv = send(full_qkv, CORE)

    flags = jnp.concatenate([near[72, :512].reshape(2, SEQ), cross[72, :512].reshape(2, SEQ)], axis=0)
    rows, cols = doc_numbers(flags)
    cosine, sine = rope_tables()

    packed = jnp.dot(hidden, full_qkv, preferred_element_type=F32)
    heads, mixture = attention(packed, rows, cols, cosine, sine)
    other_mixture = send(mixture[512:], CORE)
    other_mixture, upstream = lax.optimization_barrier((other_mixture, upstream))
    projected = jnp.dot(mixture[:512], own_out, preferred_element_type=F32)
    projected = projected + jnp.dot(other_mixture, other_out, preferred_element_type=F32)

    post_back = jax.vjp(lambda values: normalize(values, post_gain), projected)[1]
    grad_proj = post_back(upstream.astype(F32))[0].astype(BF16)
    other_mix = send(dot_nt(grad_proj, other_out).astype(BF16), CORE)
    grad_mix = jnp.concatenate([dot_nt(grad_proj, own_out).astype(BF16), other_mix], axis=0)
    both_proj = jnp.concatenate([grad_proj, send(grad_proj, CORE)], axis=0)
    partial_out = dot_tn(mixture, both_proj).astype(BF16).reshape(4, 4, 32, 2304)
    left = jnp.concatenate([partial_out[..., :1024], pack_rest(partial_out[..., 2048:])], axis=2)
    left, right = parts_of(left, 1, z), parts_of(partial_out[..., 1024:2048], 0, x)
    left_got, right_got = first_round(left, "z", 3), first_round(right, "x", 3)
    grad_mix, other_qkv = lax.optimization_barrier((grad_mix, other_qkv, *left, *right))[:2]
    grad_heads = attention_back(heads, grad_mix, rows, cols, cosine, sine)
    other_heads = send(grad_heads[512:], CORE)
    partial_qkv = dot_tn(hidden, grad_heads).astype(BF16).reshape(2, 4, 4, 72, 1024)
    near = [
        lax.dynamic_slice(partial_qkv, (core, 0, (z + d) & 3, 0, 0), (1, 4, 1, 72, 1024)).reshape(4, 72, 1024)
        for d in range(4)
    ]
    cross = [
        lax.dynamic_slice(partial_qkv, (1 - core, (x + d) & 3, 0, 0, 0), (1, 1, 4, 72, 1024)).reshape(4, 72, 1024)
        for d in range(4)
    ]
    near, cross, left_got, right_got, other_heads = lax.optimization_barrier(
        (near, cross, left_got, right_got, other_heads)
    )

    near_got, cross_got = first_round(near, "z", 1), first_round(cross, "x", 1)
    grad_rows = input_grad(
        after(grad_heads, *near, *cross), other_heads, full_qkv, other_qkv, own_tokens, upstream, norm_gain
    )
    near, cross, left, right, near_got, cross_got, grad_rows = lax.optimization_barrier(
        (near, cross, left, right, near_got, cross_got, grad_rows)
    )
    grad_rows = send(grad_rows, TRADE_BACK)
    near_far, left_far = second_round(near, near_got, "z", 1), second_round(left, left_got, "z", 3)
    cross_far, right_far = second_round(cross, cross_got, "x", 1), second_round(right, right_got, "x", 3)

    near_line = jnp.concatenate([total(near[0], near_got[1], near_far), total(left[0], left_got[1], left_far)], axis=1)
    cross_line = jnp.concatenate(
        [total(cross[0], cross_got[1], cross_far), total(right[0], right_got[1], right_far)], axis=1
    )
    sum_near = collect(parts_of(near_line, 0, x), "x")
    sum_cross = collect(parts_of(cross_line, 0, z), "z")
    sum_near, sum_cross, grad_rows = lax.optimization_barrier((sum_near, sum_cross, grad_rows))

    sum_near = send(jnp.concatenate([sum_near, sum_cross[72:]], axis=0), TRADE_BACK)
    sum_cross = send(sum_cross[:72], TRADE_CROSS)
    sum_out = jnp.concatenate([sum_near[72:104], sum_near[112:], unpack_rest(sum_near[104:112])], axis=1)
    sum_out = lax.optimization_barrier(sum_out).astype(F32)
    sum_near = sum_near[:72]
    sum_qkv = whole_columns(
        jnp.where(y_lo == 0, sum_near, sum_cross), jnp.where(y_lo == 0, sum_cross, sum_near)
    )
    sum_qkv = lax.optimization_barrier(sum_qkv).astype(F32)

    steps_done = float(SYNC_EVERY)
    inner_qkv, next_first_qkv, next_second_qkv = adam_step(
        part_qkv, sum_qkv / TOKENS, first_qkv[0], second_qkv[0], steps_done
    )
    inner_out, next_first_out, next_second_out = adam_step(
        part_out, sum_out / TOKENS, first_out[0], second_out[0], steps_done
    )
    change_qkv = (anchor_qkv - inner_qkv).astype(BF16)
    change_out = (anchor_out - inner_out).astype(BF16)
    change_rest = jnp.pad(pack_rest(change_out[:, 2048:]), ((0, 0), (0, 1024)))
    change = jnp.concatenate([change_qkv, change_out[:, :2048], change_rest], axis=0)
    pseudo = over_replicas(change)
    pseudo_qkv = pseudo[:72]
    pseudo_out = jnp.concatenate([pseudo[72:104], unpack_rest(pseudo[104:, :1024])], axis=1)
    outer_next_qkv = MOMENTUM * outer_qkv + pseudo_qkv
    outer_next_out = MOMENTUM * outer_out + pseudo_out
    anchor_next_qkv = anchor_qkv - OUTER_LR * (pseudo_qkv + MOMENTUM * outer_next_qkv)
    anchor_next_out = anchor_out - OUTER_LR * (pseudo_out + MOMENTUM * outer_next_out)
    grad_rows = jnp.where(place_fsdp < 32, grad_rows, jnp.zeros_like(grad_rows))
    return (
        grad_rows[None],
        next_first_qkv[None],
        next_first_out[None],
        next_second_qkv[None],
        next_second_out[None],
        anchor_next_qkv,
        anchor_next_out,
        outer_next_qkv,
        outer_next_out,
    )


def solution(mesh):
    rows = P("replica", "fsdp", None)
    shared = P("fsdp", None)
    in_specs = (rows, P("replica", "fsdp"), rows, P(), P(), rows, rows, shared, shared, rows, rows, rows, rows, shared, shared)
    out_specs = (rows, rows, rows, rows, rows, shared, shared, shared, shared)
    return jax.shard_map(per_device, mesh=mesh, in_specs=in_specs, out_specs=out_specs, check_vma=False)
```

```python
import functools

import jax
import jax.numpy as jnp
from jax import lax
from jax.experimental import pallas as pl
from jax.experimental.pallas import tpu as pltpu
from jax.sharding import PartitionSpec as P

HD = 256
SEQ = 256
SYNC_EVERY = 16
TOKENS = 16384

EPS_NORM = 1e-06
SOFTCAP = 50.0
ROPE_BASE = 10000.0
BETA_ONE = 0.9
BETA_TWO = 0.95
EPS_ADAM = 1e-08
INNER_LR = 0.001
DECAY = 0.1
OUTER_LR = 0.7
MOMENTUM = 0.9
START_ID = 2

BF16 = jnp.bfloat16
F32 = jnp.float32


def place(step):
    pairs = []
    for source in range(128):
        y_lo, x, z, y_hi, core = source // 64, source // 16 % 4, source // 4 % 4, source // 2 % 2, source % 2
        y_lo, x, z, y_hi, core = step(y_lo, x, z, y_hi, core)
        pairs.append((source, (((y_lo * 4 + x) * 4 + z) * 2 + y_hi) * 2 + core))
    return pairs


TRADE = place(lambda y, x, z, h, c: (1 - c, x, z, h, y))
TRADE_BACK = place(lambda y, x, z, h, c: (c, x, z, h, 1 - y))
TRADE_CROSS = place(lambda y, x, z, h, c: (1 - c, x, z, h, 1 - y))
CORE = place(lambda y, x, z, h, c: (y, x, z, h, 1 - c))
FAR = place(lambda y, x, z, h, c: (y, x, z, 1 - h, c))
RING = {
    "x": {d: place(lambda y, x, z, h, c, d=d: (y, (x + d) % 4, z, h, c)) for d in (1, 2, 3)},
    "z": {d: place(lambda y, x, z, h, c, d=d: (y, x, (z + d) % 4, h, c)) for d in (1, 2, 3)},
}


def send(values, pairs):
    return lax.ppermute(values, ("fsdp", "replica"), pairs)


def group_columns(values, group):
    return jnp.concatenate(
        [
            values[:, 512 * group : 512 * group + 512],
            values[:, 1024 + 256 * group : 1280 + 256 * group],
            values[:, 1536 + 256 * group : 1792 + 256 * group],
        ],
        axis=1,
    )


def whole_columns(first, second):
    return jnp.concatenate(
        [
            first[:, :512],
            second[:, :512],
            first[:, 512:768],
            second[:, 512:768],
            first[:, 768:],
            second[:, 768:],
        ],
        axis=1,
    )


def normalize(values, gain):
    return values * lax.rsqrt(jnp.mean(values * values, axis=-1, keepdims=True) + EPS_NORM) * gain


def rope_tables():
    freqs = ROPE_BASE ** (-2.0 * jnp.arange(HD // 2, dtype=F32) / HD)
    angles = jnp.arange(SEQ, dtype=F32)[:, None] * freqs[None, :]
    return jnp.cos(angles), jnp.sin(angles)


def doc_numbers(flags):
    ordered = (jnp.arange(SEQ)[:, None] <= jnp.arange(SEQ)[None, :]).astype(BF16)
    numbers = jnp.dot(flags, ordered, preferred_element_type=F32)
    return numbers[:, None, :], numbers[:, :, None]


def doc_mask(row_ref, col_ref):
    same_doc = col_ref[0] == row_ref[0]
    places = (SEQ, SEQ)
    causal = lax.broadcasted_iota(jnp.int32, places, 1) <= lax.broadcasted_iota(jnp.int32, places, 0)
    return same_doc & causal


def rotated(values, cosine, sine):
    first, second = values[:, : HD // 2], values[:, HD // 2 :]
    return jnp.concatenate(
        [first * cosine - second * sine, second * cosine + first * sine], axis=1
    ).astype(BF16)


def rotated_back(grads, cosine, sine):
    grads = grads.astype(BF16).astype(F32)
    first, second = grads[:, : HD // 2], grads[:, HD // 2 :]
    return jnp.concatenate(
        [first * cosine + second * sine, second * cosine - first * sine], axis=1
    ).astype(BF16)


def dot_nt(left, right):
    return lax.dot_general(left, right, (((1,), (1,)), ((), ())), preferred_element_type=F32)


def dot_tn(left, right):
    return lax.dot_general(left, right, (((0,), (0,)), ((), ())), preferred_element_type=F32)


def chance(query, key, mask):
    capped = jnp.tanh(dot_nt(query, key) * (HD**-0.5 / SOFTCAP))
    weights = jnp.where(mask, jnp.exp(SOFTCAP * capped), 0.0)
    return capped, weights / jnp.sum(weights, axis=1, keepdims=True)


def attention_kernel(packed_ref, row_ref, col_ref, cos_ref, sin_ref, heads_ref, mixture_ref):
    mask = doc_mask(row_ref, col_ref)
    cosine, sine = cos_ref[...], sin_ref[...]
    key = rotated(packed_ref[:, 512:768], cosine, sine)
    value = packed_ref[:, 768:].astype(BF16)
    heads_ref[:, 512:768] = key
    heads_ref[:, 768:] = value
    for head in range(2):
        columns = slice(head * HD, head * HD + HD)
        query = rotated(packed_ref[:, columns], cosine, sine)
        heads_ref[:, columns] = query
        chances = chance(query, key, mask)[1].astype(BF16)
        mixture_ref[:, columns] = jnp.dot(chances, value, preferred_element_type=F32).astype(BF16)


def attention_back_kernel(heads_ref, grad_ref, row_ref, col_ref, cos_ref, sin_ref, out_ref):
    mask = doc_mask(row_ref, col_ref)
    cosine, sine = cos_ref[...], sin_ref[...]
    key, value = heads_ref[:, 512:768], heads_ref[:, 768:]
    grad_key = jnp.zeros((SEQ, HD), F32)
    grad_value = jnp.zeros((SEQ, HD), F32)
    for head in range(2):
        columns = slice(head * HD, head * HD + HD)
        query, grad = heads_ref[:, columns], grad_ref[:, columns]
        capped, chances = chance(query, key, mask)
        grad_chance = dot_nt(grad, value).astype(BF16).astype(F32)
        inner = jnp.sum(grad_chance * chances, axis=1, keepdims=True)
        grad_score = chances * (grad_chance - inner) * (1.0 - capped * capped) * HD**-0.5
        grad_score = grad_score.astype(BF16)
        grad_query = jnp.dot(grad_score, key, preferred_element_type=F32)
        out_ref[:, columns] = rotated_back(grad_query, cosine, sine)
        grad_key += dot_tn(grad_score, query)
        grad_value += dot_tn(chances.astype(BF16), grad)
    out_ref[:, 512:768] = rotated_back(grad_key, cosine, sine)
    out_ref[:, 768:] = grad_value.astype(BF16)


def per_sequence(width):
    return pl.BlockSpec((SEQ, width), lambda s: (s, 0))


DOC_SPECS = [
    pl.BlockSpec((1, 1, SEQ), lambda s: (s, 0, 0)),
    pl.BlockSpec((1, SEQ, 1), lambda s: (s, 0, 0)),
    pl.BlockSpec((SEQ, HD // 2), lambda s: (0, 0)),
    pl.BlockSpec((SEQ, HD // 2), lambda s: (0, 0)),
]
KERNEL_PARAMS = pltpu.CompilerParams(vmem_limit_bytes=12 * 1024 * 1024)


def attention(packed, rows, cols, cosine, sine):
    count = packed.shape[0]
    return pl.pallas_call(
        attention_kernel,
        grid=(count // SEQ,),
        in_specs=[per_sequence(1024)] + DOC_SPECS,
        out_specs=[per_sequence(1024), per_sequence(512)],
        out_shape=[jax.ShapeDtypeStruct((count, 1024), BF16), jax.ShapeDtypeStruct((count, 512), BF16)],
        compiler_params=KERNEL_PARAMS,
        cost_estimate=pl.CostEstimate(flops=6 * count * 1024 * SEQ, bytes_accessed=8 * count * 1024, transcendentals=4 * count * SEQ),
        name="attention",
    )(packed, rows, cols, cosine, sine)


def attention_back(heads, grads, rows, cols, cosine, sine):
    count = heads.shape[0]
    return pl.pallas_call(
        attention_back_kernel,
        grid=(count // SEQ,),
        in_specs=[per_sequence(1024), per_sequence(512)] + DOC_SPECS,
        out_specs=per_sequence(1024),
        out_shape=jax.ShapeDtypeStruct((count, 1024), BF16),
        compiler_params=KERNEL_PARAMS,
        cost_estimate=pl.CostEstimate(flops=12 * count * 1024 * SEQ, bytes_accessed=8 * count * 1024, transcendentals=4 * count * SEQ),
        name="attention_back",
    )(heads, grads, rows, cols, cosine, sine)


def norm_kernel(own_ref, other_ref, gain_ref, out_ref):
    step = pl.program_id(0)

    @pl.when(step < 2)
    def _():
        out_ref[...] = normalize(own_ref[...].astype(F32), gain_ref[...]).astype(BF16)

    @pl.when(step >= 2)
    def _():
        out_ref[...] = normalize(other_ref[...].astype(F32), gain_ref[...]).astype(BF16)


def norm_rows(own, other, gain):
    width = own.shape[1]
    return pl.pallas_call(
        norm_kernel,
        grid=(4,),
        in_specs=[
            pl.BlockSpec((256, width), lambda s: (jnp.minimum(s, 1), 0)),
            pl.BlockSpec((256, width), lambda s: (jnp.maximum(s - 2, 0), 0)),
            pl.BlockSpec((1, width), lambda s: (0, 0)),
        ],
        out_specs=pl.BlockSpec((256, width), lambda s: (s, 0)),
        out_shape=jax.ShapeDtypeStruct((1024, width), BF16),
        compiler_params=pltpu.CompilerParams(vmem_limit_bytes=16 * 1024 * 1024),
        name="norm_rows",
    )(own, other, gain[None])


def input_grad_kernel(own_ref, other_ref, near_ref, far_ref, tokens_ref, upstream_ref, gain_ref, out_ref, grad_ref):
    step = pl.program_id(0)
    columns = pl.ds(pl.multiple_of(step * 768, 256), 768)
    grad_ref[:, columns] = dot_nt(own_ref[...], near_ref[...]) + dot_nt(other_ref[...], far_ref[...])

    @pl.when(step == 2)
    def _():
        def rows_back(i, carry):
            rows = pl.ds(pl.multiple_of(i * 64, 64), 64)
            values = tokens_ref[rows, :].astype(F32)
            grads = grad_ref[rows, :] * gain_ref[...]
            scale = lax.rsqrt(jnp.mean(values * values, axis=-1, keepdims=True) + EPS_NORM)
            inner = jnp.mean(grads * values, axis=-1, keepdims=True) * scale * scale * scale
            total_grad = upstream_ref[rows, :].astype(F32) + (grads * scale - values * inner)
            out_ref[rows, :] = total_grad.astype(BF16)
            return carry

        lax.fori_loop(0, 8, rows_back, 0)


def input_grad(heads, other_heads, own_qkv, other_qkv, tokens, upstream, gain):
    count, width = tokens.shape

    def whole(shape):
        return pl.BlockSpec(shape, lambda s: (0, 0))

    return pl.pallas_call(
        input_grad_kernel,
        grid=(width // 768,),
        in_specs=[
            whole((count, 1024)),
            whole((count, 1024)),
            pl.BlockSpec((768, 1024), lambda s: (s, 0)),
            pl.BlockSpec((768, 1024), lambda s: (s, 0)),
            whole((count, width)),
            whole((count, width)),
            whole((1, width)),
        ],
        out_specs=whole((count, width)),
        out_shape=jax.ShapeDtypeStruct((count, width), BF16),
        scratch_shapes=[pltpu.VMEM((count, width), F32)],
        compiler_params=pltpu.CompilerParams(vmem_limit_bytes=40 * 1024 * 1024),
        name="input_grad",
    )(heads, other_heads, own_qkv, other_qkv, tokens, upstream, gain[None])


def after(values, *others):
    return lax.optimization_barrier((values, *others))[0]


def parts_of(values, axis, index):
    return [lax.dynamic_index_in_dim(values, (index + d) & 3, axis, keepdims=False) for d in range(4)]


def put(whole, block, start):
    return lax.dynamic_update_slice(whole, block, start)


def line_of(block, axis, index):
    line = jnp.zeros((4,) + block.shape, BF16)
    line = put(line, block[None], (index, 0, 0))
    ahead, behind = both_ways(block, axis)
    across = send(ahead, RING[axis][1])
    for step, received in ((3, ahead), (1, behind), (2, across)):
        line = put(line, received[None], ((index + step) & 3, 0, 0))
    return line


def both_ways(line, axis):
    return send(line, RING[axis][1]), send(line, RING[axis][3])


def first_round(parts, axis, way):
    return send(parts[2], RING[axis][way]), send(parts[4 - way], RING[axis][4 - way])


def second_round(parts, got, axis, way):
    return send(add(parts[way], got[0]), RING[axis][way])


def pack_rest(rest):
    return jnp.concatenate([rest[..., 8 * k : 8 * k + 8, :] for k in range(4)], axis=-1)


def unpack_rest(rest):
    return jnp.concatenate([rest[:, 256 * k : 256 * k + 256] for k in range(4)], axis=0)


def add(left, right):
    return (left.astype(F32) + right.astype(F32)).astype(BF16)


def total(*terms):
    return functools.reduce(lambda left, right: left + right, [term.astype(F32) for term in terms]).astype(BF16)


def collect(parts, axis):
    got = first_round(parts, axis, 1)
    return total(parts[0], got[1], second_round(parts, got, axis, 1))


def adam_step(weights, grads, first, second, steps_done):
    first_next = BETA_ONE * first + (1.0 - BETA_ONE) * grads
    second_next = BETA_TWO * second + (1.0 - BETA_TWO) * grads * grads
    first_hat = first_next / (1.0 - BETA_ONE**steps_done)
    second_hat = second_next / (1.0 - BETA_TWO**steps_done)
    master = weights.astype(F32)
    inner = master - INNER_LR * (first_hat / (jnp.sqrt(second_hat) + EPS_ADAM) + DECAY * master)
    return (inner, first_next, second_next)


def over_replicas(change):
    pair = add(change, send(change, CORE))
    return (pair.astype(F32) + send(pair, FAR).astype(F32)) / 4.0


def per_device(
    tokens,
    token_ids,
    cotangent,
    norm_gain,
    post_gain,
    local_qkv,
    local_out,
    anchor_qkv,
    anchor_out,
    first_qkv,
    first_out,
    second_qkv,
    second_out,
    outer_qkv,
    outer_out,
):
    place_fsdp = lax.axis_index("fsdp")
    y_lo, x, z = place_fsdp >> 4, (place_fsdp >> 2) & 3, place_fsdp & 3
    core = lax.axis_index("replica") & 1
    part_qkv, part_out = local_qkv[0], local_out[0]

    flags = (token_ids[0] == START_ID).astype(BF16).reshape(1, 512)
    flags = jnp.pad(flags, ((0, 7), (0, 512)))
    group_a, group_b = group_columns(part_qkv, 0), group_columns(part_qkv, 1)
    near = send(jnp.concatenate([jnp.where(y_lo == 0, group_a, group_b), flags], axis=0), TRADE)
    cross = send(jnp.concatenate([jnp.where(y_lo == 0, group_b, group_a), flags], axis=0), TRADE_CROSS)
    rows_out = send(part_out, TRADE)
    tokens_a, tokens_b = tokens[0, :192], tokens[0, 192:]
    near, cross, rows_out, tokens_a, tokens_b = lax.optimization_barrier(
        (near, cross, rows_out, tokens_a, tokens_b)
    )

    tokens_a = send(tokens_a, TRADE)
    near_line = line_of(near[:72], "x", x)
    cross_line = line_of(cross[:72], "z", z)
    near_line, cross_line, tokens_a = lax.optimization_barrier((near_line, cross_line, tokens_a))

    tokens_b = send(after(tokens_b, tokens_a), TRADE)
    near_up, near_down = both_ways(near_line, "z")
    cross_up, cross_down = both_ways(cross_line, "x")
    own_tokens = jnp.concatenate([tokens_a, tokens_b], axis=0)
    cotangent = after(cotangent, tokens_b)
    groups = [[16 * y + i for i in range(16)] for y in range(2)]
    own_out = lax.all_gather(rows_out, "fsdp", axis=0, tiled=True, axis_index_groups=groups)
    near_line, cross_line, near_up, near_down, cross_up, cross_down, own_tokens, own_out = lax.optimization_barrier(
        (near_line, cross_line, near_up, near_down, cross_up, cross_down, own_tokens, own_out)
    )

    near_far = send(near_up, RING["z"][1])
    cross_far = send(cross_up, RING["x"][1])
    other_tokens = send(own_tokens, CORE)
    upstream = send(cotangent[0], TRADE)
    hidden = norm_rows(own_tokens, other_tokens, norm_gain)
    whole = jnp.zeros((2, 4, 4, 72, 1024), BF16)
    for step, block in ((0, near_line), (3, near_up), (1, near_down)):
        whole = put(whole, block[None, :, None], (core, 0, (z + step) & 3, 0, 0))
    for step, block in ((0, cross_line), (3, cross_up), (1, cross_down)):
        whole = put(whole, block[None, None], (1 - core, (x + step) & 3, 0, 0, 0))
    whole, hidden, near_far, cross_far = lax.optimization_barrier((whole, hidden, near_far, cross_far))
    other_out = send(own_out, CORE)
    whole = put(whole, near_far[None, :, None], (core, 0, (z + 2) & 3, 0, 0))
    whole = put(whole, cross_far[None, None], (1 - core, (x + 2) & 3, 0, 0, 0))
    full_qkv = whole.reshape(2304, 1024)
    other_qkv = send(full_qkv, CORE)

    flags = jnp.concatenate([near[72, :512].reshape(2, SEQ), cross[72, :512].reshape(2, SEQ)], axis=0)
    rows, cols = doc_numbers(flags)
    cosine, sine = rope_tables()

    packed = jnp.dot(hidden, full_qkv, preferred_element_type=F32)
    heads, mixture = attention(packed, rows, cols, cosine, sine)
    other_mixture = send(mixture[512:], CORE)
    other_mixture, upstream = lax.optimization_barrier((other_mixture, upstream))
    projected = jnp.dot(mixture[:512], own_out, preferred_element_type=F32)
    projected = projected + jnp.dot(other_mixture, other_out, preferred_element_type=F32)

    post_back = jax.vjp(lambda values: normalize(values, post_gain), projected)[1]
    grad_proj = post_back(upstream.astype(F32))[0].astype(BF16)
    other_mix = send(dot_nt(grad_proj, other_out).astype(BF16), CORE)
    grad_mix = jnp.concatenate([dot_nt(grad_proj, own_out).astype(BF16), other_mix], axis=0)
    both_proj = jnp.concatenate([grad_proj, send(grad_proj, CORE)], axis=0)
    partial_out = dot_tn(mixture, both_proj).astype(BF16).reshape(4, 4, 32, 2304)
    left = jnp.concatenate([partial_out[..., :1024], pack_rest(partial_out[..., 2048:])], axis=2)
    left, right = parts_of(left, 1, z), parts_of(partial_out[..., 1024:2048], 0, x)
    left_got, right_got = first_round(left, "z", 3), first_round(right, "x", 3)
    grad_mix, other_qkv = lax.optimization_barrier((grad_mix, other_qkv, *left, *right))[:2]
    grad_heads = attention_back(heads, grad_mix, rows, cols, cosine, sine)
    other_heads = send(grad_heads[512:], CORE)
    partial_qkv = dot_tn(hidden, grad_heads).astype(BF16).reshape(2, 4, 4, 72, 1024)
    near = [
        lax.dynamic_slice(partial_qkv, (core, 0, (z + d) & 3, 0, 0), (1, 4, 1, 72, 1024)).reshape(4, 72, 1024)
        for d in range(4)
    ]
    cross = [
        lax.dynamic_slice(partial_qkv, (1 - core, (x + d) & 3, 0, 0, 0), (1, 1, 4, 72, 1024)).reshape(4, 72, 1024)
        for d in range(4)
    ]
    near, cross, left_got, right_got, other_heads = lax.optimization_barrier(
        (near, cross, left_got, right_got, other_heads)
    )

    near_got, cross_got = first_round(near, "z", 1), first_round(cross, "x", 1)
    grad_rows = input_grad(
        after(grad_heads, *near, *cross), other_heads, full_qkv, other_qkv, own_tokens, upstream, norm_gain
    )
    near, cross, left, right, near_got, cross_got, grad_rows = lax.optimization_barrier(
        (near, cross, left, right, near_got, cross_got, grad_rows)
    )
    grad_rows = send(grad_rows, TRADE_BACK)
    near_far, left_far = second_round(near, near_got, "z", 1), second_round(left, left_got, "z", 3)
    cross_far, right_far = second_round(cross, cross_got, "x", 1), second_round(right, right_got, "x", 3)

    near_line = jnp.concatenate([total(near[0], near_got[1], near_far), total(left[0], left_got[1], left_far)], axis=1)
    cross_line = jnp.concatenate(
        [total(cross[0], cross_got[1], cross_far), total(right[0], right_got[1], right_far)], axis=1
    )
    sum_near = collect(parts_of(near_line, 0, x), "x")
    sum_cross = collect(parts_of(cross_line, 0, z), "z")
    sum_near, sum_cross, grad_rows = lax.optimization_barrier((sum_near, sum_cross, grad_rows))

    sum_near = send(jnp.concatenate([sum_near, sum_cross[72:]], axis=0), TRADE_BACK)
    sum_cross = send(sum_cross[:72], TRADE_CROSS)
    sum_out = jnp.concatenate([sum_near[72:104], sum_near[112:], unpack_rest(sum_near[104:112])], axis=1)
    sum_out = lax.optimization_barrier(sum_out).astype(F32)
    sum_near = sum_near[:72]
    sum_qkv = whole_columns(
        jnp.where(y_lo == 0, sum_near, sum_cross), jnp.where(y_lo == 0, sum_cross, sum_near)
    )
    sum_qkv = lax.optimization_barrier(sum_qkv).astype(F32)

    steps_done = float(SYNC_EVERY)
    inner_qkv, next_first_qkv, next_second_qkv = adam_step(
        part_qkv, sum_qkv / TOKENS, first_qkv[0], second_qkv[0], steps_done
    )
    inner_out, next_first_out, next_second_out = adam_step(
        part_out, sum_out / TOKENS, first_out[0], second_out[0], steps_done
    )
    change_qkv = (anchor_qkv - inner_qkv).astype(BF16)
    change_out = (anchor_out - inner_out).astype(BF16)
    change_rest = jnp.pad(pack_rest(change_out[:, 2048:]), ((0, 0), (0, 1024)))
    change = jnp.concatenate([change_qkv, change_out[:, :2048], change_rest], axis=0)
    pseudo = over_replicas(change)
    pseudo_qkv = pseudo[:72]
    pseudo_out = jnp.concatenate([pseudo[72:104], unpack_rest(pseudo[104:, :1024])], axis=1)
    outer_next_qkv = MOMENTUM * outer_qkv + pseudo_qkv
    outer_next_out = MOMENTUM * outer_out + pseudo_out
    anchor_next_qkv = anchor_qkv - OUTER_LR * (pseudo_qkv + MOMENTUM * outer_next_qkv)
    anchor_next_out = anchor_out - OUTER_LR * (pseudo_out + MOMENTUM * outer_next_out)
    grad_rows = jnp.where(place_fsdp < 32, grad_rows, jnp.zeros_like(grad_rows))
    return (
        grad_rows[None],
        next_first_qkv[None],
        next_first_out[None],
        next_second_qkv[None],
        next_second_out[None],
        anchor_next_qkv,
        anchor_next_out,
        outer_next_qkv,
        outer_next_out,
    )


def solution(mesh):
    rows = P("replica", "fsdp", None)
    shared = P("fsdp", None)
    in_specs = (rows, P("replica", "fsdp"), rows, P(), P(), rows, rows, shared, shared, rows, rows, rows, rows, shared, shared)
    out_specs = (rows, rows, rows, rows, rows, shared, shared, shared, shared)
    return jax.shard_map(per_device, mesh=mesh, in_specs=in_specs, out_specs=out_specs, check_vma=False)
```
